256 devices in a mesh: aux: 64 (over y, z, core), orb: 4 (over x).
Axes of the slice: x: 4, y: 4, z: 8, core: 2. Of those that a mesh axis runs over, the one named last changes fastest.
Arguments:
- three_index: bfloat16 [512, 1600, 1600], P('aux', 'orb'), may hold values from -40 to 40, as said below
- density: bfloat16 [512, 1600, 160], P('aux', 'orb'), may hold values from -0.0068359375 to 0.0068359375
- hess_diag: float32 [1440, 160], replicated, may hold values from 0.5 to 4
Outputs:
- ov_new: bfloat16 [4, 512, 57600], P('orb', None, 'aux')
The draws below stay inside these ranges and needn't reach their ends.
Inputs may be any that keep to these rules, and one draw needn't show every extreme that they name: three_index[q, p, r] equals three_index[q, r, p].
All inputs are finite; a program needn't handle non-finite values.
Results may differ from the reference program's by a relative error of at most 0.0065.
Values may be sent and summed in bfloat16 or wider, within the bound.
A program may use at most 64 MiB of HBM per device.

```python
import math
import jax
import jax.numpy as jnp
from jax import lax

NO = 160
NV = 1440
NMO = 1600
NAUX = 512
OBLK = 40
N_ORB = 4


def draw_three_index(key, part):
    key = jax.random.fold_in(key, 7)

    def one_slice(index):
        sub_key = jax.random.fold_in(key, index + 2)
        raw_draw = jax.random.normal(sub_key, (NMO, NMO), jnp.float32)
        symmetric = (raw_draw + raw_draw.T) * 0.7071
        return symmetric.astype(jnp.bfloat16)
    return lax.map(one_slice, jnp.arange(NAUX, dtype=jnp.int32))


def levels(rng, shape, pieces, least, top_value):
    gain = 1.0
    for axis_at, blocks in pieces:
        steps = jax.random.uniform(jax.random.fold_in(jax.random.fold_in(rng, 6), axis_at), (blocks,), jnp.float32, least / len(pieces), top_value / len(pieces))
        gain = gain * jnp.repeat(jnp.exp(steps), shape[axis_at] // blocks).reshape((-1,) + (1,) * (len(shape) - 1 - axis_at))
    return gain


def noise(own_key, extent, spread, limit, shards=(), kind=jnp.bfloat16):
    entries = spread * jax.random.normal(own_key, extent, jnp.float32)
    if shards:
        entries = entries * levels(own_key, extent, shards, -0.22, 0.18)
    return jnp.clip(entries, -limit, limit).astype(kind)


def setup_inputs(seed: int = 0) -> dict:
    arg_keys = jax.random.split(jax.random.key(seed), 4)
    return {
        "three_index": draw_three_index(jax.random.fold_in(arg_keys[3], 71), 0),
        "density": noise(arg_keys[1], (NAUX, NMO, NO), (NAUX * NMO) ** -0.5, 0.0068359375, ((0, 64), (1, 4))),
        "hess_diag": jnp.clip(jnp.exp(jax.random.uniform(arg_keys[2], (NV, NO), jnp.float32, math.log(0.5), math.log(4.0))), 0.5, 4.0),
    }


def reference(three_index, density, hess_diag):
    highest = lax.Precision.HIGHEST

    def add_fock(total, pair):
        b_slice, d_slice = pair
        return (total + jnp.dot(b_slice.T, d_slice, preferred_element_type=jnp.float32), None)
    fock_full, _ = lax.scan(add_fock, jnp.zeros((NMO, NO), jnp.float32), (three_index, density))
    fock_vo = fock_full[NO:]
    generator = -fock_vo / hess_diag
    gen_norm = jnp.sqrt(jnp.sum(generator * generator))
    rotation = generator * jnp.minimum(1.0, math.sqrt(NO) / gen_norm)
    kmat = jnp.zeros((NMO, NMO), jnp.float32)
    kmat = kmat.at[NO:, :NO].set(rotation)
    kmat = kmat.at[:NO, NO:].set(-rotation.T)
    ident = jnp.eye(NMO, dtype=jnp.float32)
    power = ident
    unitary = ident
    for order in range(1, 5):
        power = jnp.dot(power, kmat, precision=highest) / float(order)
        unitary = unitary + power
    unitary_b = unitary.astype(jnp.bfloat16)
    occ_cols = unitary_b[:, :NO]
    vir_cols = unitary_b[:, NO:]

    def rotate_one(b_slice):
        half_rot = jnp.dot(b_slice, occ_cols, preferred_element_type=jnp.float32).astype(jnp.bfloat16)
        return jnp.dot(half_rot.T, vir_cols, preferred_element_type=jnp.float32).astype(jnp.bfloat16)
    rotated = lax.map(rotate_one, three_index)
    return jnp.transpose(rotated.reshape(NAUX, N_ORB, OBLK * NV), (1, 0, 2))
```

```python
import functools
import math

import jax
import jax.numpy as jnp
from jax import lax
from jax.experimental import pallas as pl
from jax.experimental.pallas import tpu as pltpu
from jax.sharding import PartitionSpec as P

MESH = pl.DeviceIdType.MESH
F32 = jnp.float32
BF16 = jnp.bfloat16
NT = (((1,), (1,)), ((), ()))

NO = 160
LANES = 1536
CHIPS = 32
TILES = 15

def place():
    aux = lax.axis_index("aux")
    orb = lax.axis_index("orb")
    return aux, orb, lax.rem(aux, 2), lax.div(aux, 2)


def remote(src, dst, send_sem, recv_sem, aux, orb):
    return pltpu.make_async_remote_copy(
        src_ref=src, dst_ref=dst, send_sem=send_sem, recv_sem=recv_sem,
        device_id={"aux": aux, "orb": orb}, device_id_type=MESH,
    )


def owner_of(tile, core):
    return (2 * tile + core) * 2 + core


def fock_kernel(b_hbm, d_hbm, h_hbm, g_out, bv, dv, hl, hv, acc, cs, cr, xs, xr, ys, yr, g,
                load_sem, cs_sem, cr_sem, xs_sem, xr_sem, ys_sem, yr_sem,
                gs_sem, gr_sem, gxs_sem, gxr_sem, gcs_sem, gcr_sem):
    aux, orb, core, chip = place()
    peer = aux + 1 - 2 * core
    barrier = pltpu.get_barrier_semaphore()

    loads = []
    for q in range(8):
        loads.append((
            pltpu.make_async_copy(d_hbm.at[q], dv.at[q], load_sem.at[2 * q]),
            pltpu.make_async_copy(b_hbm.at[q], bv.at[q], load_sem.at[2 * q + 1]),
        ))
        for copy in loads[-1]:
            copy.start()
    hess_load = pltpu.make_async_copy(h_hbm, hl, load_sem.at[16])
    hess_load.start()

    pl.semaphore_signal(barrier, inc=1, device_id={"aux": peer, "orb": orb}, device_id_type=MESH)
    for step in range(1, 4):
        pl.semaphore_signal(barrier, inc=1, device_id={"aux": aux, "orb": lax.rem(orb + step, 4)},
                            device_id_type=MESH)

    def greet(k, carry):
        other = lax.rem(chip + k, CHIPS) * 2 + core
        pl.semaphore_signal(barrier, inc=1, device_id={"aux": other, "orb": orb}, device_id_type=MESH)
        return carry
    lax.fori_loop(1, CHIPS, greet, 0)

    acc[3, :, 256:384] = jnp.zeros((NO, 128), F32)

    for q in range(8):
        for copy in loads[q]:
            copy.wait()
        part = jnp.dot(dv[q], bv[q, :, 128:1600], preferred_element_type=F32)
        for x in range(4):
            width = 384 if x < 3 else 320
            piece = part[:, 384 * x:384 * x + width]
            if q == 0:
                acc[x, :, :width] = piece
            else:
                acc[x, :, :width] += piece
    hess_load.wait()
    hv[:, 0:1408] = hl[:, 0:1408]
    hv[:, 1408:1536] = jnp.concatenate([hl[:, 1408:1440], jnp.ones((NO, 96), F32)], axis=1)
    pl.semaphore_wait(barrier, 35)

    other_rows = pl.ds(pl.multiple_of(80 * (1 - core), 16), 80)
    my_rows = pl.ds(pl.multiple_of(80 * core, 16), 80)
    core_copies = []
    for x in range(4):
        cs[x] = acc[x, other_rows, :].astype(BF16)
        copy = remote(cs.at[x], cr.at[x], cs_sem.at[x], cr_sem.at[x], peer, orb)
        copy.start()
        core_copies.append(copy)
    for x in range(4):
        core_copies[x].wait_recv()
        xs[x] = (acc[x, my_rows, :] + cr[x].astype(F32)).astype(BF16)
        @pl.when(orb != x)
        def _():
            remote(xs.at[x], xr.at[orb], xs_sem.at[x], xr_sem.at[orb], aux, x).start()
    total = acc[orb, my_rows, :] + cr[orb].astype(F32)
    for step in range(1, 4):
        src = lax.rem(orb + step, 4)
        remote(xs.at[src], xr.at[src], xs_sem.at[src], xr_sem.at[src], aux, src).wait_recv()
        total = total + xr[src].astype(F32)
    for k in range(5):
        for t in range(3):
            ys[3 * k + t] = total[16 * k:16 * k + 16, 128 * t:128 * t + 128].astype(BF16)

    def send_tile(k, carry):
        tile = lax.rem(chip + k, TILES)
        target = owner_of(tile, core)
        @pl.when(target != aux)
        def _():
            remote(ys.at[tile], yr.at[chip], ys_sem.at[tile], yr_sem.at[chip], target, orb).start()
        return carry
    lax.fori_loop(0, TILES, send_tile, 0)

    my_tile = lax.div(chip, 2)
    owner = jnp.logical_and(lax.rem(chip, 2) == core, my_tile < TILES)
    lane_tile = orb * 3 + lax.rem(my_tile, 3)

    @pl.when(owner)
    def _():
        hess_rows = pl.ds(pl.multiple_of(80 * core + 16 * lax.div(my_tile, 3), 16), 16)
        before = hv[hess_rows, pl.ds(pl.multiple_of(jnp.maximum(lane_tile - 1, 0) * 128, 128), 128)]
        after = hv[hess_rows, pl.ds(pl.multiple_of(lane_tile * 128, 128), 128)]
        in_tile = lax.broadcasted_iota(jnp.int32, (16, 128), 1)
        hess = pltpu.roll(jnp.where(in_tile < 96, after, before), 32, 1)
        yr[chip] = ys[my_tile]

        def wait_tile(k, carry):
            src = lax.rem(chip + k, CHIPS)
            remote(ys.at[0], yr.at[src], ys_sem.at[0], yr_sem.at[src], aux, orb).wait_recv()
            return carry
        lax.fori_loop(1, CHIPS, wait_tile, 0)
        fock = yr[0].astype(F32)
        for src in range(1, CHIPS):
            fock = fock + yr[src].astype(F32)
        lane = lane_tile * 128 + in_tile
        valid = jnp.logical_and(lane >= 32, lane < 1472)
        g[core, orb, my_tile] = jnp.where(valid, -fock / hess, 0.0).astype(BF16)

        def spread(k, carry):
            other = lax.rem(chip + k, CHIPS)
            mine = g.at[core, orb, my_tile]
            remote(mine, mine, gs_sem.at[other], gr_sem.at[my_tile], other * 2 + core, orb).start()
            return carry
        lax.fori_loop(1, CHIPS, spread, 0)

    def gather_tile(tile, carry):
        @pl.when(owner_of(tile, core) != aux)
        def _():
            there = g.at[core, orb, tile]
            remote(there, there, gs_sem.at[0], gr_sem.at[tile], aux, orb).wait_recv()
        return carry
    lax.fori_loop(0, TILES, gather_tile, 0)

    own = g.at[core, orb]
    for step in (1, 3, 2):
        x = lax.rem(orb + step, 4)
        remote(own, own, gxs_sem.at[x], gxr_sem.at[orb], aux, x).start()
    remote(own, own, gcs_sem.at[orb], gcr_sem.at[orb], peer, orb).start()
    for step in (1, 3, 2):
        x = lax.rem(orb + step, 4)
        there = g.at[core, x]
        remote(there, there, gxs_sem.at[x], gxr_sem.at[x], aux, x).wait_recv()
        remote(there, there, gcs_sem.at[x], gcr_sem.at[x], peer, orb).start()
    for x in range(4):
        there = g.at[1 - core, x]
        remote(there, there, gcs_sem.at[x], gcr_sem.at[x], peer, orb).wait_recv()
    g_out[...] = g[...]

    for x in range(4):
        core_copies[x].wait_send()
        there = g.at[core, x]
        remote(there, there, gcs_sem.at[x], gcr_sem.at[x], peer, orb).wait_send()
        @pl.when(orb != x)
        def _():
            remote(xs.at[x], xr.at[orb], xs_sem.at[x], xr_sem.at[orb], aux, x).wait_send()
            remote(own, own, gxs_sem.at[x], gxr_sem.at[orb], aux, x).wait_send()

    def sent_tile(tile, carry):
        target = owner_of(tile, core)
        @pl.when(target != aux)
        def _():
            remote(ys.at[tile], yr.at[chip], ys_sem.at[tile], yr_sem.at[chip], target, orb).wait_send()
        return carry
    lax.fori_loop(0, TILES, sent_tile, 0)

    @pl.when(owner)
    def _():
        def sent(k, carry):
            other = lax.rem(chip + k, CHIPS)
            mine = g.at[core, orb, my_tile]
            remote(mine, mine, gs_sem.at[other], gr_sem.at[my_tile], other * 2 + core, orb).wait_send()
            return carry
        lax.fori_loop(1, CHIPS, sent, 0)


def rotate_kernel(g_ref, b_hbm, out, bv, rt, gb, u, left, lx, hs, hb, hr, rot, ob,
                  load_sem, hs_sem, hr_sem, os_sem, or_sem):
    aux, orb, core, chip = place()
    barrier = pltpu.get_barrier_semaphore()
    loads = []
    for q in range(8):
        copy = pltpu.make_async_copy(b_hbm.at[q], bv.at[q], load_sem.at[q])
        copy.start()
        loads.append(copy)

    near = [(0, 1)] + [(step, flip) for step in (1, 3, 2) for flip in (0, 1)]
    def near_device(step, flip):
        other_core = core + flip - 2 * core * flip
        return 2 * chip + other_core, lax.rem(orb + step, 4), other_core
    for step, flip in near:
        to_aux, to_orb, _ = near_device(step, flip)
        pl.semaphore_signal(barrier, inc=1, device_id={"aux": to_aux, "orb": to_orb}, device_id_type=MESH)
    source_core = lax.div(aux, 32)

    def greet(k, carry):
        other = 2 * lax.rem(chip + k, CHIPS) + source_core
        @pl.when(other != aux)
        def _():
            pl.semaphore_signal(barrier, inc=1, device_id={"aux": other, "orb": orb}, device_id_type=MESH)
        return carry
    lax.fori_loop(0, CHIPS, greet, 0)

    for c in range(2):
        for x in range(4):
            for k in range(5):
                for t in range(3):
                    tile = g_ref[c, x, 3 * k + t]
                    lanes = 384 * x + 128 * t
                    gb[80 * c + 16 * k:80 * c + 16 * k + 16, lanes:lanes + 128] = tile
    gb[NO:, :] = jnp.zeros((256 - NO, LANES), BF16)
    gen = gb[0:NO, :].astype(F32)
    norm = jnp.sqrt(jnp.sum(gen * gen, axis=(0, 1), keepdims=True))
    scale = jnp.minimum(1.0, math.sqrt(NO) / norm)
    gram = lax.dot_general(gb[...], gb[...], NT, preferred_element_type=F32)
    inter = gram * (scale * scale)
    inter_b = inter.astype(BF16)
    squared = jnp.dot(inter_b[:NO], inter_b, preferred_element_type=F32)
    over = jnp.dot(inter_b[:NO], gb[...], preferred_element_type=F32) * scale
    rotation = gen * scale
    inter = inter[:NO]
    eye = jnp.where(lax.broadcasted_iota(jnp.int32, (NO, 256), 0)
                    == lax.broadcasted_iota(jnp.int32, (NO, 256), 1), 1.0, 0.0)
    occ = eye - inter / 2.0 + squared / 24.0
    occ_left = inter / 6.0 - eye
    vir = rotation - over / 6.0
    vir_left = over / 24.0 - rotation / 2.0
    early = lax.broadcasted_iota(jnp.int32, (NO, 128), 1) < 32
    u[:, 0:128] = occ[:, 0:128].astype(BF16)
    u[:, 128:256] = jnp.where(early, occ[:, 128:256], vir[:, 0:128]).astype(BF16)
    u[:, 256:1664] = vir[:, 128:1536].astype(BF16)
    left[:, 0:128] = occ_left[:, 0:128]
    left[:, 128:256] = jnp.where(early, occ_left[:, 128:256], vir_left[:, 0:128])
    left[:, 256:1664] = vir_left[:, 128:1536]
    own_lanes = lax.broadcasted_iota(jnp.int32, (NO, 512), 1) < 400
    for x in range(4):
        window = left[:, 384 * x:384 * x + 512]
        if x:
            window = pltpu.roll(window, 512 - 16 * x, 1)
        lx[x] = jnp.where(own_lanes, window, 0.0).astype(BF16)

    pad = jnp.zeros((NO, 112), F32)
    for q in range(8):
        loads[q].wait()
        half = lax.dot_general(u[:, 0:1600], bv[q], NT, preferred_element_type=F32)
        half = jnp.concatenate([half, pad], axis=1)
        for t in range(4):
            hs[t, pl.ds(q, NO, stride=8), :] = half[:, 128 * t:128 * t + 128]
    for t in range(4):
        hb[:, 128 * t:128 * t + 128] = hs[t].astype(BF16)
    waits = 39 - (source_core == core).astype(jnp.int32)
    pl.semaphore_wait(barrier, waits)
    copies = []
    for n, (step, flip) in enumerate(near):
        to_aux, to_orb, to_core = near_device(step, flip)
        rows = pl.ds(pl.multiple_of(160 * (2 * to_orb + to_core), 16), 160)
        copy = remote(hb.at[rows], hr.at[orb, core], hs_sem.at[n], hr_sem.at[2 * orb + core], to_aux, to_orb)
        copy.start()
        copies.append(copy)
    hr[orb, core] = hb[pl.ds(pl.multiple_of(160 * (2 * orb + core), 16), 160), :]
    for step, flip in near:
        _, from_orb, from_core = near_device(step, flip)
        there = hr.at[from_orb, from_core]
        remote(there, there, hs_sem.at[0], hr_sem.at[2 * from_orb + from_core], aux, orb).wait_recv()

    held = [jnp.concatenate([hr[x, 0], hr[x, 1]], axis=0) for x in range(4)]
    mid = lax.dot_general(held[0], lx[0], NT, preferred_element_type=F32)
    for x in range(1, 4):
        mid = mid + lax.dot_general(held[x], lx[x], NT, preferred_element_type=F32)
    rot[...] = jnp.dot((mid * scale).astype(BF16), gb[0:NO, :], preferred_element_type=F32)
    rot[:, 0:384] += held[0][:, 128:512].astype(F32)
    for x, lanes in ((1, 256), (2, 640), (3, 1024)):
        rot[:, lanes:lanes + 512] += pltpu.roll(held[x].astype(F32), 16 * x, 1)

    lane = lax.broadcasted_iota(jnp.int32, (16, 1024), 1)
    for d in range(32):
        j, first = divmod(900 * d, 1440)
        def rows_of(i):
            return jnp.concatenate([rot[8 * i:8 * i + 8, :], rot[160 + 8 * i:168 + 8 * i, :]], axis=0)
        block = pltpu.roll(rows_of(j), LANES - 32 - first, 1)[:, :1024]
        count = min(900, 1440 - first)
        if count < 900:
            block = jnp.where(lane < count, block, pltpu.roll(rows_of(j + 1), count - 32, 1)[:, :1024])
        ob[d] = block.astype(BF16)

    out_rows = pl.ds(pl.multiple_of(16 * chip, 16), 16)

    def send_block(k, carry):
        d = lax.rem(chip + k, 32)
        target = 32 * core + d
        @pl.when(target != aux)
        def _():
            remote(ob.at[d], out.at[out_rows], os_sem.at[d], or_sem.at[chip], target, orb).start()
        @pl.when(target == aux)
        def _():
            pltpu.make_async_copy(ob.at[d], out.at[out_rows], or_sem.at[chip]).start()
        return carry
    lax.fori_loop(0, 32, send_block, 0)

    def land(src, carry):
        rows = pl.ds(pl.multiple_of(16 * src, 16), 16)
        pltpu.make_async_copy(ob.at[0], out.at[rows], or_sem.at[src]).wait()
        return carry
    lax.fori_loop(0, CHIPS, land, 0)

    def sent(d, carry):
        target = 32 * core + d
        @pl.when(target != aux)
        def _():
            remote(ob.at[d], out.at[out_rows], os_sem.at[d], or_sem.at[chip], target, orb).wait_send()
        return carry
    lax.fori_loop(0, 32, sent, 0)
    for copy in copies:
        copy.wait_send()


DMA = pltpu.SemaphoreType.DMA
ANY = pl.BlockSpec(memory_space=pl.ANY)
VM = pl.BlockSpec(memory_space=pltpu.VMEM)


def lay_out_kernel(x_ref, o_ref):
    for t in range(4):
        o_ref[:, 128 * t:128 * t + 128] = x_ref[128 * t:128 * t + 128, :].T[:900]


def on_device(three_index, density, hess_diag):
    gen = pl.pallas_call(
        fock_kernel,
        out_shape=jax.ShapeDtypeStruct((2, 4, TILES, 16, 128), BF16),
        in_specs=[ANY, ANY, ANY],
        out_specs=VM,
        scratch_shapes=[
            pltpu.VMEM((8, 400, 1600), BF16),
            pltpu.VMEM((8, NO, 400), BF16),
            pltpu.VMEM((NO, 1440), F32),
            pltpu.VMEM((NO, LANES), F32),
            pltpu.VMEM((4, NO, 384), F32),
            pltpu.VMEM((4, 80, 384), BF16),
            pltpu.VMEM((4, 80, 384), BF16),
            pltpu.VMEM((4, 80, 384), BF16),
            pltpu.VMEM((4, 80, 384), BF16),
            pltpu.VMEM((TILES, 16, 128), BF16),
            pltpu.VMEM((CHIPS, 16, 128), BF16),
            pltpu.VMEM((2, 4, TILES, 16, 128), BF16),
            DMA((17,)),
            DMA((4,)), DMA((4,)), DMA((4,)), DMA((4,)),
            DMA((TILES,)), DMA((CHIPS,)),
            DMA((CHIPS,)), DMA((TILES,)),
            DMA((4,)), DMA((4,)), DMA((4,)), DMA((4,)),
        ],
        compiler_params=pltpu.CompilerParams(
            collective_id=0, has_side_effects=True, vmem_limit_bytes=60 * 1024 * 1024),
        name="fock_reduce",
    )(three_index, jnp.transpose(density, (0, 2, 1)), hess_diag.T)
    out = pl.pallas_call(
        rotate_kernel,
        out_shape=jax.ShapeDtypeStruct((512, 1024), BF16),
        in_specs=[VM, ANY],
        out_specs=ANY,
        scratch_shapes=[
            pltpu.VMEM((8, 400, 1600), BF16),
            pltpu.VMEM((NO, LANES), F32),
            pltpu.VMEM((256, LANES), BF16),
            pltpu.VMEM((NO, 1664), BF16),
            pltpu.VMEM((NO, 1664), F32),
            pltpu.VMEM((4, NO, 512), BF16),
            pltpu.VMEM((4, 1280, 128), F32),
            pltpu.VMEM((1280, 512), BF16),
            pltpu.VMEM((4, 2, NO, 512), BF16),
            pltpu.VMEM((320, LANES), F32),
            pltpu.VMEM((32, 16, 1024), BF16),
            DMA((8,)),
            DMA((7,)), DMA((8,)),
            DMA((32,)), DMA((CHIPS,)),
        ],
        compiler_params=pltpu.CompilerParams(
            collective_id=1, has_side_effects=True, vmem_limit_bytes=60 * 1024 * 1024),
        name="rotate_exchange",
    )(gen, three_index)
    pairs = pl.pallas_call(
        lay_out_kernel,
        out_shape=jax.ShapeDtypeStruct((900, 512), BF16),
        in_specs=[VM],
        out_specs=VM,
        name="lay_out",
    )(out)
    return pairs.T[None]


def solution(mesh):
    return jax.shard_map(
        on_device,
        mesh=mesh,
        in_specs=(P("aux", "orb", None), P("aux", "orb", None), P()),
        out_specs=P("orb", None, "aux"),
        check_vma=False,
    )
```

```python
import functools
import math

import jax
import jax.numpy as jnp
from jax import lax
from jax.experimental import pallas as pl
from jax.experimental.pallas import tpu as pltpu
from jax.sharding import PartitionSpec as P

MESH = pl.DeviceIdType.MESH
F32 = jnp.float32
BF16 = jnp.bfloat16
NT = (((1,), (1,)), ((), ()))

NO = 160
LANES = 1536
CHIPS = 32
TILES = 15
PHASES = 2
QP = 8 // PHASES
CUT = 448
FAR_FIRST = sorted(
    ((dy, dz) for dy in range(4) for dz in range(8) if dy or dz),
    key=lambda at: -(min(at[0], 4 - at[0]) + min(at[1], 8 - at[1])),
)


def place():
    aux = lax.axis_index("aux")
    orb = lax.axis_index("orb")
    return aux, orb, lax.rem(aux, 2), lax.div(aux, 2)


def remote(src, dst, send_sem, recv_sem, aux, orb):
    return pltpu.make_async_remote_copy(
        src_ref=src, dst_ref=dst, send_sem=send_sem, recv_sem=recv_sem,
        device_id={"aux": aux, "orb": orb}, device_id_type=MESH,
    )


def owner_of(tile, core):
    return (2 * tile + core) * 2 + core


def kernel(b_hbm, d_hbm, h_hbm, out, bv, dv, hl, hv, acc, cs, cr, xs, xr, ys, yr, g,
           gb, u, left, lx, hs, hb, hr, hx, rot, rc, ob, rv,
           load_sem, cs_sem, cr_sem, xs_sem, xr_sem, ys_sem, yr_sem,
           gs_sem, gr_sem, gxs_sem, gxr_sem, gcs_sem, gcr_sem,
           hs_sem, hr_sem, os_sem, or_sem):
    aux, orb, core, chip = place()
    peer = aux + 1 - 2 * core
    barrier = pltpu.get_barrier_semaphore()

    loads = []
    for q in range(8):
        loads.append((
            pltpu.make_async_copy(d_hbm.at[q], dv.at[q], load_sem.at[2 * q]),
            pltpu.make_async_copy(b_hbm.at[q], bv.at[q], load_sem.at[2 * q + 1]),
        ))
        for copy in loads[-1]:
            copy.start()
    hess_load = pltpu.make_async_copy(h_hbm, hl, load_sem.at[16])
    hess_load.start()

    pl.semaphore_signal(barrier, inc=1, device_id={"aux": peer, "orb": orb}, device_id_type=MESH)
    for step in range(1, 4):
        pl.semaphore_signal(barrier, inc=1, device_id={"aux": aux, "orb": lax.rem(orb + step, 4)},
                            device_id_type=MESH)

    def greet(k, carry):
        other = lax.rem(chip + k, CHIPS) * 2 + core
        pl.semaphore_signal(barrier, inc=1, device_id={"aux": other, "orb": orb}, device_id_type=MESH)
        return carry
    lax.fori_loop(1, CHIPS, greet, 0)

    near = [(0, 1)] + [(step, flip) for step in (1, 3, 2) for flip in (0, 1)]

    def near_device(step, flip):
        other_core = core + flip - 2 * core * flip
        return 2 * chip + other_core, lax.rem(orb + step, 4), other_core
    waits = 35

    g[:, :, TILES] = jnp.zeros((2, 4, 16, 128), BF16)
    acc[3, :, 256:384] = jnp.zeros((NO, 128), F32)

    for q in range(8):
        for copy in loads[q]:
            copy.wait()
        part = jnp.dot(dv[q], bv[q, :, 128:1600], preferred_element_type=F32)
        for x in range(4):
            width = 384 if x < 3 else 320
            piece = part[:, 384 * x:384 * x + width]
            if q == 0:
                acc[x, :, :width] = piece
            else:
                acc[x, :, :width] += piece
    hess_load.wait()
    hv[:, 0:1408] = hl[:, 0:1408]
    hv[:, 1408:1536] = jnp.concatenate([hl[:, 1408:1440], jnp.ones((NO, 96), F32)], axis=1)
    pl.semaphore_wait(barrier, waits)

    other_rows = pl.ds(pl.multiple_of(80 * (1 - core), 16), 80)
    my_rows = pl.ds(pl.multiple_of(80 * core, 16), 80)
    core_copies = []
    for x in range(4):
        cs[x] = acc[x, other_rows, :].astype(BF16)
        copy = remote(cs.at[x], cr.at[x], cs_sem.at[x], cr_sem.at[x], peer, orb)
        copy.start()
        core_copies.append(copy)
    for x in range(4):
        core_copies[x].wait_recv()
        xs[x] = (acc[x, my_rows, :] + cr[x].astype(F32)).astype(BF16)
        @pl.when(orb != x)
        def _():
            remote(xs.at[x], xr.at[orb], xs_sem.at[x], xr_sem.at[orb], aux, x).start()
    total = acc[orb, my_rows, :] + cr[orb].astype(F32)
    for step in range(1, 4):
        src = lax.rem(orb + step, 4)
        remote(xs.at[src], xr.at[src], xs_sem.at[src], xr_sem.at[src], aux, src).wait_recv()
        total = total + xr[src].astype(F32)
    for k in range(5):
        for t in range(3):
            ys[3 * k + t] = total[16 * k:16 * k + 16, 128 * t:128 * t + 128].astype(BF16)

    row, z = lax.div(chip, 8), lax.rem(chip, 8)
    for step_y in (2, 1, 3, 0):
        for step_z in (2, 1, 3, 0):
            tile = 4 * lax.rem(row + step_y, 4) + lax.rem(lax.div(z, 2) + step_z, 4)
            target = owner_of(tile, core)
            @pl.when(jnp.logical_and(tile < TILES, target != aux))
            def _():
                remote(ys.at[tile], yr.at[chip], ys_sem.at[tile], yr_sem.at[chip], target, orb).start()

    my_tile = lax.div(chip, 2)
    owner = jnp.logical_and(lax.rem(chip, 2) == core, my_tile < TILES)
    lane_tile = orb * 3 + lax.rem(my_tile, 3)

    @pl.when(owner)
    def _():
        hess_rows = pl.ds(pl.multiple_of(80 * core + 16 * lax.div(my_tile, 3), 16), 16)
        before = hv[hess_rows, pl.ds(pl.multiple_of(jnp.maximum(lane_tile - 1, 0) * 128, 128), 128)]
        after = hv[hess_rows, pl.ds(pl.multiple_of(lane_tile * 128, 128), 128)]
        in_tile = lax.broadcasted_iota(jnp.int32, (16, 128), 1)
        hess = pltpu.roll(jnp.where(in_tile < 96, after, before), 32, 1)
        yr[chip] = ys[my_tile]

        def wait_tile(k, carry):
            src = lax.rem(chip + k, CHIPS)
            remote(ys.at[0], yr.at[src], ys_sem.at[0], yr_sem.at[src], aux, orb).wait_recv()
            return carry
        lax.fori_loop(1, CHIPS, wait_tile, 0)
        fock = yr[0].astype(F32)
        for src in range(1, CHIPS):
            fock = fock + yr[src].astype(F32)
        lane = lane_tile * 128 + in_tile
        valid = jnp.logical_and(lane >= 32, lane < 1472)
        g[core, orb, my_tile] = jnp.where(valid, -fock / hess, 0.0).astype(BF16)

        mine = g.at[core, orb, my_tile]
        for step_y, step_z in FAR_FIRST:
            other = 8 * lax.rem(row + step_y, 4) + lax.rem(z + step_z, 8)
            remote(mine, mine, gs_sem.at[other], gr_sem.at[my_tile], other * 2 + core, orb).start()

    groups = [lax.rem(row + step, 4) for step in (0, 1, 3, 2)]
    for group in groups:
        for n in range(4):
            tile = 4 * group + n
            @pl.when(jnp.logical_and(tile < TILES, owner_of(tile, core) != aux))
            def _():
                there = g.at[core, orb, tile]
                remote(there, there, gs_sem.at[0], gr_sem.at[tile], aux, orb).wait_recv()
        own = g.at[core, orb, pl.ds(4 * group, 4)]
        for step in (2, 1, 3):
            x = lax.rem(orb + step, 4)
            remote(own, own, gxs_sem.at[x, group], gxr_sem.at[orb, group], aux, x).start()
        remote(own, own, gcs_sem.at[orb, group], gcr_sem.at[orb, group], peer, orb).start()
    for group in groups:
        for step in (1, 3, 2):
            x = lax.rem(orb + step, 4)
            there = g.at[core, x, pl.ds(4 * group, 4)]
            remote(there, there, gxs_sem.at[x, group], gxr_sem.at[x, group], aux, x).wait_recv()
            remote(there, there, gcs_sem.at[x, group], gcr_sem.at[x, group], peer, orb).start()
    for group in groups:
        for step in (0, 1, 3, 2):
            x = lax.rem(orb + step, 4)
            there = g.at[1 - core, x, pl.ds(4 * group, 4)]
            remote(there, there, gcs_sem.at[x, group], gcr_sem.at[x, group], peer, orb).wait_recv()

    for c in range(2):
        for x in range(4):
            for k in range(5):
                for t in range(3):
                    tile = g[c, x, 3 * k + t]
                    lanes = 384 * x + 128 * t
                    gb[80 * c + 16 * k:80 * c + 16 * k + 16, lanes:lanes + 128] = tile
    gb[NO:, :] = jnp.zeros((256 - NO, LANES), BF16)
    gen = gb[0:NO, :].astype(F32)
    norm = jnp.sqrt(jnp.sum(gen * gen, axis=(0, 1), keepdims=True))
    scale = jnp.minimum(1.0, math.sqrt(NO) / norm)
    gram = lax.dot_general(gb[...], gb[...], NT, preferred_element_type=F32)
    inter = gram * (scale * scale)
    inter_b = inter.astype(BF16)
    squared = jnp.dot(inter_b[:NO], inter_b, preferred_element_type=F32)
    over = jnp.dot(inter_b[:NO], gb[...], preferred_element_type=F32) * scale
    rotation = gen * scale
    inter = inter[:NO]
    eye = jnp.where(lax.broadcasted_iota(jnp.int32, (NO, 256), 0)
                    == lax.broadcasted_iota(jnp.int32, (NO, 256), 1), 1.0, 0.0)
    occ = eye - inter / 2.0 + squared / 24.0
    occ_left = inter / 6.0 - eye
    vir = rotation - over / 6.0
    vir_left = over / 24.0 - rotation / 2.0
    early = lax.broadcasted_iota(jnp.int32, (NO, 128), 1) < 32
    u[:, 0:128] = occ[:, 0:128].astype(BF16)
    u[:, 128:256] = jnp.where(early, occ[:, 128:256], vir[:, 0:128]).astype(BF16)
    u[:, 256:1664] = vir[:, 128:1536].astype(BF16)
    left[:, 0:128] = occ_left[:, 0:128]
    left[:, 128:256] = jnp.where(early, occ_left[:, 128:256], vir_left[:, 0:128])
    left[:, 256:1664] = vir_left[:, 128:1536]
    own_lanes = lax.broadcasted_iota(jnp.int32, (NO, 512), 1) < 400
    for x in range(4):
        window = left[:, 384 * x:384 * x + 512]
        if x:
            window = pltpu.roll(window, 512 - 16 * x, 1)
        lx[x] = jnp.where(own_lanes, window, 0.0).astype(BF16)

    pad = jnp.zeros((NO, 112), F32)
    copies = []

    def send_half(p, n):
        to_aux, to_orb, to_core = near_device(*near[n])
        copy = remote(hb.at[p, 2 * to_orb + to_core], hr.at[p, 2 * orb + core], hs_sem.at[p, n],
                      hr_sem.at[p, 2 * orb + core], to_aux, to_orb)
        copy.start()
        copies.append(copy)

    for p in range(PHASES):
        for n in range(QP):
            half = lax.dot_general(u[:, 0:1600], bv[QP * p + n], NT, preferred_element_type=F32)
            half = jnp.concatenate([half, pad], axis=1)
            for t in range(4):
                hs[4 * p + t, pl.ds(n, NO, stride=QP), :] = half[:, 128 * t:128 * t + 128]
        for dest in range(8):
            last = None
            for k in range(5):
                rows = pl.ds(80 * dest + 16 * k, 16)
                for t in range(3):
                    hb[p, dest, 3 * k + t] = hs[4 * p + t, rows, :].astype(BF16)
                piece = hs[4 * p + 3, rows, :]
                last = piece if last is None else last + pltpu.roll(piece, 16 * k, 1)
            hb[p, dest, 15] = last.astype(BF16)
        if p == 0:
            for n in range(7):
                send_half(0, n)
        hr[p, 2 * orb + core] = hb[p, 2 * orb + core]

    tail_lanes = lax.broadcasted_iota(jnp.int32, (16, 128), 1) < 16
    upper = lax.broadcasted_iota(jnp.int32, (8, LANES), 0) < 4
    lane = lax.broadcasted_iota(jnp.int32, (8, 512), 1)

    def block(start, size):
        j, first = divmod(start, 1440)
        count = min(size, 1440 - first)
        low = min((32 + first) // 128 * 128, LANES - 640)
        found = pltpu.roll(rc[j, :, low:low + 640], (640 - 32 - first + low) % 640, 1)[:, :512]
        if count < size:
            more = pltpu.roll(rc[j + 1, :, 0:640], (count - 32) % 640, 1)[:, :512]
            found = jnp.where(lane < count, found, more)
        return found

    def send_block(p, d, near_by):
        target = 32 * core + d

        def go():
            remote(ob.at[p, d], rv.at[p, chip], os_sem.at[p, d], or_sem.at[p, chip], target, orb).start()
        if near_by:
            pl.when(target != aux)(go)
            @pl.when(target == aux)
            def _():
                pltpu.make_async_copy(ob.at[p, d], rv.at[p, chip], or_sem.at[p, chip]).start()
        else:
            go()

    for p in range(PHASES):
        for step, flip in near:
            _, from_orb, from_core = near_device(step, flip)
            there = hr.at[p, 2 * from_orb + from_core]
            remote(there, there, hs_sem.at[p, 0], hr_sem.at[p, 2 * from_orb + from_core], aux, orb).wait_recv()
        for x in range(4):
            for c in range(2):
                last = hr[p, 2 * x + c, 15].astype(F32)
                for k in range(5):
                    rows = pl.ds(80 * c + 16 * k, 16)
                    for t in range(3):
                        hx[x, rows, 128 * t:128 * t + 128] = hr[p, 2 * x + c, 3 * k + t]
                    piece = pltpu.roll(last, (128 - 16 * k) % 128, 1) if k else last
                    hx[x, rows, 384:512] = jnp.where(tail_lanes, piece, 0.0).astype(BF16)
        mid = lax.dot_general(hx[0], lx[0], NT, preferred_element_type=F32)
        for x in range(1, 4):
            mid = mid + lax.dot_general(hx[x], lx[x], NT, preferred_element_type=F32)
        rot[...] = jnp.dot((mid * scale).astype(BF16), gb[0:NO, :], preferred_element_type=F32)
        rot[:, 0:384] += hx[0, :, 128:512].astype(F32)
        for x, lanes in ((1, 256), (2, 640), (3, 1024)):
            rot[:, lanes:lanes + 512] += pltpu.roll(hx[x].astype(F32), 16 * x, 1)
        for m in range(10):
            first_core = rot[8 * m:8 * m + 8, :]
            second_core = rot[80 + 8 * m:88 + 8 * m, :]
            rc[2 * m] = jnp.where(upper, first_core, pltpu.roll(second_core, 4, 0))
            rc[2 * m + 1] = jnp.where(upper, pltpu.roll(first_core, 4, 0), second_core)
        for d in range(32):
            ob[p, d] = jnp.concatenate(
                [block(900 * d, CUT), block(900 * d + CUT, 900 - CUT)], axis=0).astype(BF16)

        for turn, step_z in enumerate((4, 3, 5, 2, 6, 1, 7, 0)):
            if p + 1 < PHASES and turn < 7:
                send_half(p + 1, turn)
            for half_y in range(2):
                for to_core in range(2):
                    d = 16 * half_y + 2 * lax.rem(z + step_z, 8) + to_core
                    send_block(p, d, step_z == 0)

    def lay_out(k, carry):
        group = lax.rem(row + k, 4)

        def land(n, inner):
            for p in range(PHASES):
                there = rv.at[p, 8 * group + n]
                pltpu.make_async_copy(ob.at[p, 0], there, or_sem.at[p, 8 * group + n]).wait()
            return inner
        lax.fori_loop(0, 8, land, 0)
        lanes = pl.ds(pl.multiple_of(128 * group, 128), 128)
        for h in range(2):
            found = []
            for n in range(8):
                early = rv[0, 8 * group + n, 8 * h:8 * h + 8, :].astype(F32)
                late = rv[1, 8 * group + n, 8 * h:8 * h + 8, :].astype(F32)
                found.append(jnp.where(upper[:, :512], early, pltpu.roll(late, 4, 0)))
                found.append(jnp.where(upper[:, :512], pltpu.roll(early, 4, 0), late))
            turned = jnp.concatenate(found, axis=0).T.astype(BF16)
            if h == 0:
                out[0:CUT, lanes] = turned[:CUT]
            else:
                out[CUT:900, lanes] = turned[:900 - CUT]
        return carry
    lax.fori_loop(0, 4, lay_out, 0)

    for x in range(4):
        core_copies[x].wait_send()
        for group in range(4):
            there = g.at[core, x, pl.ds(4 * group, 4)]
            remote(there, there, gcs_sem.at[x, group], gcr_sem.at[x, group], peer, orb).wait_send()
        @pl.when(orb != x)
        def _():
            remote(xs.at[x], xr.at[orb], xs_sem.at[x], xr_sem.at[orb], aux, x).wait_send()
            for group in range(4):
                own = g.at[core, orb, pl.ds(4 * group, 4)]
                remote(own, own, gxs_sem.at[x, group], gxr_sem.at[orb, group], aux, x).wait_send()

    def sent_tile(tile, carry):
        target = owner_of(tile, core)
        @pl.when(target != aux)
        def _():
            remote(ys.at[tile], yr.at[chip], ys_sem.at[tile], yr_sem.at[chip], target, orb).wait_send()
        return carry
    lax.fori_loop(0, TILES, sent_tile, 0)

    @pl.when(owner)
    def _():
        def sent(k, carry):
            other = lax.rem(chip + k, CHIPS)
            mine = g.at[core, orb, my_tile]
            remote(mine, mine, gs_sem.at[other], gr_sem.at[my_tile], other * 2 + core, orb).wait_send()
            return carry
        lax.fori_loop(1, CHIPS, sent, 0)

    def sent_block(d, carry):
        target = 32 * core + d
        @pl.when(target != aux)
        def _():
            for p in range(PHASES):
                remote(ob.at[p, d], rv.at[p, chip], os_sem.at[p, d], or_sem.at[p, chip], target, orb).wait_send()
        return carry
    lax.fori_loop(0, 32, sent_block, 0)
    for copy in copies:
        copy.wait_send()


DMA = pltpu.SemaphoreType.DMA
ANY = pl.BlockSpec(memory_space=pl.ANY)
VM = pl.BlockSpec(memory_space=pltpu.VMEM)


def on_device(three_index, density, hess_diag):
    pairs = pl.pallas_call(
        kernel,
        out_shape=jax.ShapeDtypeStruct((900, 512), BF16),
        in_specs=[ANY, ANY, ANY],
        out_specs=VM,
        scratch_shapes=[
            pltpu.VMEM((8, 400, 1600), BF16),
            pltpu.VMEM((8, NO, 400), BF16),
            pltpu.VMEM((NO, 1440), F32),
            pltpu.VMEM((NO, LANES), F32),
            pltpu.VMEM((4, NO, 384), F32),
            pltpu.VMEM((4, 80, 384), BF16),
            pltpu.VMEM((4, 80, 384), BF16),
            pltpu.VMEM((4, 80, 384), BF16),
            pltpu.VMEM((4, 80, 384), BF16),
            pltpu.VMEM((TILES, 16, 128), BF16),
            pltpu.VMEM((CHIPS, 16, 128), BF16),
            pltpu.VMEM((2, 4, 16, 16, 128), BF16),
            pltpu.VMEM((256, LANES), BF16),
            pltpu.VMEM((NO, 1664), BF16),
            pltpu.VMEM((NO, 1664), F32),
            pltpu.VMEM((4, NO, 512), BF16),
            pltpu.VMEM((4 * PHASES, NO * QP, 128), F32),
            pltpu.VMEM((PHASES, 8, 16, 16, 128), BF16),
            pltpu.VMEM((PHASES, 8, 16, 16, 128), BF16),
            pltpu.VMEM((4, 160, 512), BF16),
            pltpu.VMEM((160, LANES), F32),
            pltpu.VMEM((20, 8, LANES), F32),
            pltpu.VMEM((PHASES, 32, 16, 512), BF16),
            pltpu.VMEM((PHASES, CHIPS, 16, 512), BF16),
            DMA((17,)),
            DMA((4,)), DMA((4,)), DMA((4,)), DMA((4,)),
            DMA((TILES,)), DMA((CHIPS,)),
            DMA((CHIPS,)), DMA((TILES,)),
            DMA((4, 4)), DMA((4, 4)), DMA((4, 4)), DMA((4, 4)),
            DMA((PHASES, 7)), DMA((PHASES, 8)),
            DMA((PHASES, 32)), DMA((PHASES, CHIPS)),
        ],
        compiler_params=pltpu.CompilerParams(
            collective_id=0, has_side_effects=True, vmem_limit_bytes=53 * 1024 * 1024),
        name="rotate",
    )(three_index, jnp.transpose(density, (0, 2, 1)), hess_diag.T)
    return pairs.T[None]


def solution(mesh):
    return jax.shard_map(
        on_device,
        mesh=mesh,
        in_specs=(P("aux", "orb", None), P("aux", "orb", None), P()),
        out_specs=P("orb", None, "aux"),
        check_vma=False,
    )
```

```python
import functools
import math

import jax
import jax.numpy as jnp
from jax import lax
from jax.experimental import pallas as pl
from jax.experimental.pallas import tpu as pltpu
from jax.sharding import PartitionSpec as P

MESH = pl.DeviceIdType.MESH
F32 = jnp.float32
BF16 = jnp.bfloat16
NT = (((1,), (1,)), ((), ()))

NO = 160
LANES = 1536
CHIPS = 32
TILES = 15
PHASES = 2
QP = 8 // PHASES

def place():
    aux = lax.axis_index("aux")
    orb = lax.axis_index("orb")
    return aux, orb, lax.rem(aux, 2), lax.div(aux, 2)


def remote(src, dst, send_sem, recv_sem, aux, orb):
    return pltpu.make_async_remote_copy(
        src_ref=src, dst_ref=dst, send_sem=send_sem, recv_sem=recv_sem,
        device_id={"aux": aux, "orb": orb}, device_id_type=MESH,
    )


def kernel(b_hbm, d_hbm, h_hbm, out, bv, dv, hl, hv, acc, cs, cr, xs, xr, ys, yr, zr, g,
           gb, u, left, lx, hs, hb, hr, hx, rot, rc, ob, oc, lo, kept, rv, rw, lr, rest_rows,
           load_sem, cs_sem, cr_sem, xs_sem, xr_sem, ys_sem, yr_sem, zs_sem, zr_sem,
           gs_sem, gr_sem, gxs_sem, gxr_sem, gcs_sem, gcr_sem,
           hs_sem, hr_sem, os_sem, or_sem):
    aux, orb, core, chip = place()
    peer = aux + 1 - 2 * core
    barrier = pltpu.get_barrier_semaphore()

    loads = []
    for q in range(8):
        loads.append((
            pltpu.make_async_copy(d_hbm.at[q], dv.at[q], load_sem.at[2 * q]),
            pltpu.make_async_copy(b_hbm.at[q], bv.at[q], load_sem.at[2 * q + 1]),
        ))
        for copy in loads[-1]:
            copy.start()
    hess_load = pltpu.make_async_copy(h_hbm, hl, load_sem.at[16])
    hess_load.start()

    pl.semaphore_signal(barrier, inc=1, device_id={"aux": peer, "orb": orb}, device_id_type=MESH)
    for step in range(1, 4):
        pl.semaphore_signal(barrier, inc=1, device_id={"aux": aux, "orb": lax.rem(orb + step, 4)},
                            device_id_type=MESH)

    for step in range(1, 4):
        other = lax.rem(lax.div(chip, 8) + step, 4) * 8 + lax.rem(chip, 8)
        pl.semaphore_signal(barrier, inc=1, device_id={"aux": 2 * other + core, "orb": orb}, device_id_type=MESH)
    for step in range(1, 8):
        other = lax.div(chip, 8) * 8 + lax.rem(chip + step, 8)
        pl.semaphore_signal(barrier, inc=1, device_id={"aux": 2 * other + core, "orb": orb}, device_id_type=MESH)

    near = [(0, 1)] + [(step, flip) for step in (2, 1, 3) for flip in (0, 1)]

    def near_device(step, flip):
        other_core = core + flip - 2 * core * flip
        return 2 * chip + other_core, lax.rem(orb + step, 4), other_core

    g[:, :, TILES] = jnp.zeros((2, 4, 16, 128), BF16)
    ys[TILES] = jnp.zeros((16, 128), BF16)
    acc[3, :, 256:384] = jnp.zeros((NO, 128), F32)

    for q in range(8):
        for copy in loads[q]:
            copy.wait()
        part = jnp.dot(dv[q], bv[q, :, 128:1600], preferred_element_type=F32)
        for x in range(4):
            width = 384 if x < 3 else 320
            piece = part[:, 384 * x:384 * x + width]
            if q == 0:
                acc[x, :, :width] = piece
            else:
                acc[x, :, :width] += piece
    hess_load.wait()
    hv[:, 0:1408] = hl[:, 0:1408]
    hv[:, 1408:1536] = jnp.concatenate([hl[:, 1408:1440], jnp.ones((NO, 96), F32)], axis=1)
    pl.semaphore_wait(barrier, 14)

    other_rows = pl.ds(pl.multiple_of(80 * (1 - core), 16), 80)
    my_rows = pl.ds(pl.multiple_of(80 * core, 16), 80)
    core_copies = []
    order = [lax.rem(orb + step, 4) for step in (2, 1, 3, 0)]
    for x in order:
        cs[x] = acc[x, other_rows, :].astype(BF16)
        copy = remote(cs.at[x], cr.at[x], cs_sem.at[x], cr_sem.at[x], peer, orb)
        copy.start()
        core_copies.append(copy)
    x_copies = []
    for n, x in enumerate(order[:3]):
        core_copies[n].wait_recv()
        xs[x] = (acc[x, my_rows, :] + cr[x].astype(F32)).astype(BF16)
        copy = remote(xs.at[x], xr.at[orb], xs_sem.at[x], xr_sem.at[orb], aux, x)
        copy.start()
        x_copies.append(copy)
    core_copies[3].wait_recv()
    total = acc[orb, my_rows, :] + cr[orb].astype(F32)
    for step in range(1, 4):
        src = lax.rem(orb + step, 4)
        remote(xs.at[src], xr.at[src], xs_sem.at[src], xr_sem.at[src], aux, src).wait_recv()
        total = total + xr[src].astype(F32)
    for k in range(5):
        for t in range(3):
            ys[3 * k + t] = total[16 * k:16 * k + 16, 128 * t:128 * t + 128].astype(BF16)

    row, z = lax.div(chip, 8), lax.rem(chip, 8)
    yz_copies = []
    for step in (2, 1, 3):
        other = lax.rem(row + step, 4)
        copy = remote(ys.at[pl.ds(4 * other, 4)], yr.at[row], ys_sem.at[step], yr_sem.at[row],
                      (8 * other + z) * 2 + core, orb)
        copy.start()
        yz_copies.append(copy)
    yr[row] = ys[pl.ds(4 * row, 4)]
    for step in (1, 3, 2):
        src = lax.rem(row + step, 4)
        remote(yr.at[src], yr.at[src], ys_sem.at[0], yr_sem.at[src], aux, orb).wait_recv()
    fock = yr[0].astype(F32)
    for src in range(1, 4):
        fock = fock + yr[src].astype(F32)
    zr[z] = fock.astype(BF16)

    for step in (4, 3, 5, 2, 6, 1, 7):
        far = lax.rem(z + step, 8)
        copy = remote(zr.at[z], zr.at[z], zs_sem.at[step], zr_sem.at[z], (8 * row + far) * 2 + core, orb)
        copy.start()
        yz_copies.append(copy)
    hess = []
    in_tile = lax.broadcasted_iota(jnp.int32, (16, 128), 1)
    for n in range(4):
        tile = jnp.minimum(4 * row + n, TILES - 1)
        lane_tile = orb * 3 + lax.rem(tile, 3)
        hess_rows = pl.ds(pl.multiple_of(80 * core + 16 * lax.div(tile, 3), 16), 16)
        before = hv[hess_rows, pl.ds(pl.multiple_of(jnp.maximum(lane_tile - 1, 0) * 128, 128), 128)]
        after = hv[hess_rows, pl.ds(pl.multiple_of(lane_tile * 128, 128), 128)]
        lane = lane_tile * 128 + in_tile
        valid = jnp.logical_and(lane >= 32, lane < 1472)
        hess.append((valid, pltpu.roll(jnp.where(in_tile < 96, after, before), 32, 1)))
    for step in (1, 7, 2, 6, 3, 5, 4):
        src = lax.rem(z + step, 8)
        remote(zr.at[src], zr.at[src], zs_sem.at[0], zr_sem.at[src], aux, orb).wait_recv()
    for n in range(4):
        fock = zr[0, n].astype(F32)
        for src in range(1, 8):
            fock = fock + zr[src, n].astype(F32)
        valid, tile_hess = hess[n]
        @pl.when(4 * row + n < TILES)
        def _():
            g[core, orb, 4 * row + n] = jnp.where(valid, -fock / tile_hess, 0.0).astype(BF16)

    own = g.at[core, orb, pl.ds(4 * row, 4)]
    for step in (2, 1, 3):
        other = lax.rem(row + step, 4)
        copy = remote(own, own, gs_sem.at[step], gr_sem.at[row], (8 * other + z) * 2 + core, orb)
        copy.start()
        yz_copies.append(copy)
    groups = [lax.rem(row + step, 4) for step in (0, 1, 3, 2)]
    for n, group in enumerate(groups):
        own = g.at[core, orb, pl.ds(4 * group, 4)]
        if n:
            remote(own, own, gs_sem.at[0], gr_sem.at[group], aux, orb).wait_recv()
        for step in (2, 1, 3):
            x = lax.rem(orb + step, 4)
            remote(own, own, gxs_sem.at[x, group], gxr_sem.at[orb, group], aux, x).start()
        remote(own, own, gcs_sem.at[orb, group], gcr_sem.at[orb, group], peer, orb).start()
    for group in groups:
        for step in (1, 3, 2):
            x = lax.rem(orb + step, 4)
            there = g.at[core, x, pl.ds(4 * group, 4)]
            remote(there, there, gxs_sem.at[x, group], gxr_sem.at[x, group], aux, x).wait_recv()
            remote(there, there, gcs_sem.at[x, group], gcr_sem.at[x, group], peer, orb).start()
    for group in groups:
        for step in (0, 1, 3, 2):
            x = lax.rem(orb + step, 4)
            there = g.at[1 - core, x, pl.ds(4 * group, 4)]
            remote(there, there, gcs_sem.at[x, group], gcr_sem.at[x, group], peer, orb).wait_recv()

    for c in range(2):
        for x in range(4):
            for k in range(5):
                for t in range(3):
                    tile = g[c, x, 3 * k + t]
                    lanes = 384 * x + 128 * t
                    gb[80 * c + 16 * k:80 * c + 16 * k + 16, lanes:lanes + 128] = tile
    gb[NO:, :] = jnp.zeros((256 - NO, LANES), BF16)
    gen = gb[0:NO, :].astype(F32)
    norm = jnp.sqrt(jnp.sum(gen * gen, axis=(0, 1), keepdims=True))
    scale = jnp.minimum(1.0, math.sqrt(NO) / norm)
    gram = lax.dot_general(gb[...], gb[...], NT, preferred_element_type=F32)
    inter = gram * (scale * scale)
    inter_b = inter.astype(BF16)
    squared = jnp.dot(inter_b[:NO], inter_b, preferred_element_type=F32)
    over = jnp.dot(inter_b[:NO], gb[...], preferred_element_type=F32) * scale
    rotation = gen * scale
    inter = inter[:NO]
    eye = jnp.where(lax.broadcasted_iota(jnp.int32, (NO, 256), 0)
                    == lax.broadcasted_iota(jnp.int32, (NO, 256), 1), 1.0, 0.0)
    occ = eye - inter / 2.0 + squared / 24.0
    occ_left = inter / 6.0 - eye
    vir = rotation - over / 6.0
    vir_left = over / 24.0 - rotation / 2.0
    early = lax.broadcasted_iota(jnp.int32, (NO, 128), 1) < 32
    u[:, 0:128] = occ[:, 0:128].astype(BF16)
    u[:, 128:256] = jnp.where(early, occ[:, 128:256], vir[:, 0:128]).astype(BF16)
    u[:, 256:1664] = vir[:, 128:1536].astype(BF16)
    left[:, 0:128] = occ_left[:, 0:128]
    left[:, 128:256] = jnp.where(early, occ_left[:, 128:256], vir_left[:, 0:128])
    left[:, 256:1664] = vir_left[:, 128:1536]
    own_lanes = lax.broadcasted_iota(jnp.int32, (NO, 512), 1) < 400
    for x in range(4):
        window = left[:, 384 * x:384 * x + 512]
        if x:
            window = pltpu.roll(window, 512 - 16 * x, 1)
        lx[x] = jnp.where(own_lanes, window, 0.0).astype(BF16)

    pad = jnp.zeros((NO, 112), F32)
    copies = []

    def send_half(p, n):
        to_aux, to_orb, to_core = near_device(*near[n])
        copy = remote(hb.at[p, 2 * to_orb + to_core], hr.at[p, 2 * orb + core], hs_sem.at[p, n],
                      hr_sem.at[p, 2 * orb + core], to_aux, to_orb)
        copy.start()
        copies.append(copy)

    for p in range(PHASES):
        for n in range(QP):
            half = lax.dot_general(u[:, 0:1600], bv[QP * p + n], NT, preferred_element_type=F32)
            half = jnp.concatenate([half, pad], axis=1)
            for t in range(4):
                hs[4 * p + t, pl.ds(n, NO, stride=QP), :] = half[:, 128 * t:128 * t + 128]
        for dest in range(8):
            last = None
            for k in range(5):
                rows = pl.ds(80 * dest + 16 * k, 16)
                for t in range(3):
                    hb[p, dest, 3 * k + t] = hs[4 * p + t, rows, :].astype(BF16)
                piece = hs[4 * p + 3, rows, :]
                last = piece if last is None else last + pltpu.roll(piece, 16 * k, 1)
            hb[p, dest, 15] = last.astype(BF16)
        for n in range(7):
            send_half(p, n)
        hr[p, 2 * orb + core] = hb[p, 2 * orb + core]

    tail_lanes = lax.broadcasted_iota(jnp.int32, (16, 128), 1) < 16
    upper = lax.broadcasted_iota(jnp.int32, (8, 128), 0) < 4
    upper_all = lax.broadcasted_iota(jnp.int32, (8, LANES), 0) < 4
    lane = lax.broadcasted_iota(jnp.int32, (8, 1024), 1)

    def block(d):
        j, first = divmod(900 * d, 1440)
        count = min(900, 1440 - first)
        found = pltpu.roll(rc[j], (LANES - 32 - first) % LANES, 1)[:, :1024]
        if count < 900:
            found = jnp.where(lane < count, found, pltpu.roll(rc[j + 1], (count - 32) % LANES, 1)[:, :1024])
        return found

    def row_of_rest(found, p):
        rest = jnp.where(lane[:, :128] < 4, found[:, 896:1024], 0.0)
        return jnp.sum(pltpu.roll(rest, 32 * p, 1, stride=4, stride_axis=0), axis=0, keepdims=True)

    def send_block(p, d, near_by):
        target = 32 * core + d

        routes = [(ob.at[d], rv.at[chip])] if p == 0 else [(oc.at[d], rw.at[chip]), (lo.at[d], lr.at[chip])]

        def go():
            for n, (src, dst) in enumerate(routes):
                remote(src, dst, os_sem.at[p + n, d], or_sem.at[p + n, chip], target, orb).start()
        if near_by:
            pl.when(target != aux)(go)
            @pl.when(target == aux)
            def _():
                for n, (src, dst) in enumerate(routes):
                    pltpu.make_async_copy(src, dst, or_sem.at[p + n, chip]).start()
        else:
            go()

    for p in range(PHASES):
        for step, flip in near:
            _, from_orb, from_core = near_device(step, flip)
            there = hr.at[p, 2 * from_orb + from_core]
            remote(there, there, hs_sem.at[p, 0], hr_sem.at[p, 2 * from_orb + from_core], aux, orb).wait_recv()
        for x in range(4):
            for c in range(2):
                last = hr[p, 2 * x + c, 15].astype(F32)
                for k in range(5):
                    rows = pl.ds(80 * c + 16 * k, 16)
                    for t in range(3):
                        hx[x, rows, 128 * t:128 * t + 128] = hr[p, 2 * x + c, 3 * k + t]
                    piece = pltpu.roll(last, (128 - 16 * k) % 128, 1) if k else last
                    hx[x, rows, 384:512] = jnp.where(tail_lanes, piece, 0.0).astype(BF16)
        mid = lax.dot_general(hx[0], lx[0], NT, preferred_element_type=F32)
        for x in range(1, 4):
            mid = mid + lax.dot_general(hx[x], lx[x], NT, preferred_element_type=F32)
        rot[...] = jnp.dot((mid * scale).astype(BF16), gb[0:NO, :], preferred_element_type=F32)
        rot[:, 0:384] += hx[0, :, 128:512].astype(F32)
        for x, lanes in ((1, 256), (2, 640), (3, 1024)):
            rot[:, lanes:lanes + 512] += pltpu.roll(hx[x].astype(F32), 16 * x, 1)
        for m in range(10):
            first_core = rot[8 * m:8 * m + 8, :]
            second_core = rot[80 + 8 * m:88 + 8 * m, :]
            rc[2 * m] = jnp.where(upper_all, first_core, pltpu.roll(second_core, 4, 0))
            rc[2 * m + 1] = jnp.where(upper_all, pltpu.roll(first_core, 4, 0), second_core)
        for d in range(32):
            found = block(d)
            if p == 0:
                ob[d] = jnp.concatenate([found[:, 0:384], found[:, 384:768]], axis=0).astype(BF16)
                kept[d] = found[:, 768:896]
                lo[d] = row_of_rest(found, 0)
            else:
                second = jnp.concatenate([found[:, 512:896], kept[d]], axis=1)
                oc[d] = jnp.concatenate([found[:, 0:512], second], axis=0).astype(BF16)
                lo[d] += row_of_rest(found, 1)
        for turn, step_z in enumerate((4, 3, 5, 2, 6, 1, 7, 0)):
            for half_y in range(2):
                for to_core in range(2):
                    d = 16 * half_y + 2 * lax.rem(z + step_z, 8) + to_core
                    send_block(p, d, step_z == 0)

    def lay_out(k, carry):
        group = lax.rem(row + k, 4)

        def land(n, inner):
            src = 8 * group + n
            for n, (block_of, there) in enumerate(((ob, rv), (oc, rw), (lo, lr))):
                pltpu.make_async_copy(block_of.at[0], there.at[src], or_sem.at[n, src]).wait()
            rest_rows[pl.ds(src, 1), :] = lr[src]
            return inner
        lax.fori_loop(0, 8, land, 0)
        lanes = pl.ds(pl.multiple_of(128 * group, 128), 128)
        for t in range(7):
            found = []
            for n in range(8):
                src = 8 * group + n
                if t < 3:
                    early = rv[src, 0:8, 128 * t:128 * t + 128]
                elif t < 6:
                    early = rv[src, 8:16, 128 * t - 384:128 * t - 256]
                else:
                    early = rw[src, 8:16, 384:512]
                if t < 4:
                    late = rw[src, 0:8, 128 * t:128 * t + 128]
                else:
                    late = rw[src, 8:16, 128 * t - 512:128 * t - 384]
                early, late = early.astype(F32), late.astype(F32)
                found.append(jnp.where(upper, early, pltpu.roll(late, 4, 0)))
                found.append(jnp.where(upper, pltpu.roll(early, 4, 0), late))
            out[128 * t:128 * t + 128, lanes] = jnp.concatenate(found, axis=0).T.astype(BF16)
        return carry
    lax.fori_loop(0, 4, lay_out, 0)

    at, turn = lax.broadcasted_iota(jnp.int32, (512, 128), 0), lax.broadcasted_iota(jnp.int32, (512, 128), 1)
    chips = lax.broadcasted_iota(jnp.int32, (512, 32), 1)
    spread = jnp.where(lax.broadcasted_iota(jnp.int32, (512, 32), 0) // 16 == chips, 1.0, 0.0).astype(BF16)
    wide = jnp.dot(spread, rest_rows[...].astype(BF16), preferred_element_type=F32)
    wanted = 8 * (at // 4 % 2) + 4 * (at // 8 % 2) + at % 4
    wide = jnp.where(turn // 4 == wanted, wide, 0.0).astype(BF16)
    column = lax.broadcasted_iota(jnp.int32, (16, 128), 0)
    pick = jnp.where(lax.broadcasted_iota(jnp.int32, (16, 128), 1) % 4 == column, 1.0, 0.0).astype(BF16)
    rest = lax.dot_general(pick, wide, NT, preferred_element_type=F32)
    out[896:900, :] = rest[0:4].astype(BF16)

    for copy in core_copies + x_copies + yz_copies:
        copy.wait_send()
    for x in range(4):
        for group in range(4):
            there = g.at[core, x, pl.ds(4 * group, 4)]
            remote(there, there, gcs_sem.at[x, group], gcr_sem.at[x, group], peer, orb).wait_send()
        @pl.when(orb != x)
        def _():
            for group in range(4):
                own = g.at[core, orb, pl.ds(4 * group, 4)]
                remote(own, own, gxs_sem.at[x, group], gxr_sem.at[orb, group], aux, x).wait_send()

    def sent_block(d, carry):
        target = 32 * core + d
        @pl.when(target != aux)
        def _():
            for n, (src, dst) in enumerate(((ob, rv), (oc, rw), (lo, lr))):
                remote(src.at[d], dst.at[chip], os_sem.at[n, d], or_sem.at[n, chip], target, orb).wait_send()
        return carry
    lax.fori_loop(0, 32, sent_block, 0)
    for copy in copies:
        copy.wait_send()


DMA = pltpu.SemaphoreType.DMA
ANY = pl.BlockSpec(memory_space=pl.ANY)
VM = pl.BlockSpec(memory_space=pltpu.VMEM)


def on_device(three_index, density, hess_diag):
    pairs = pl.pallas_call(
        kernel,
        out_shape=jax.ShapeDtypeStruct((900, 512), BF16),
        in_specs=[ANY, ANY, ANY],
        out_specs=VM,
        scratch_shapes=[
            pltpu.VMEM((8, 400, 1600), BF16),
            pltpu.VMEM((8, NO, 400), BF16),
            pltpu.VMEM((NO, 1440), F32),
            pltpu.VMEM((NO, LANES), F32),
            pltpu.VMEM((4, NO, 384), F32),
            pltpu.VMEM((4, 80, 384), BF16),
            pltpu.VMEM((4, 80, 384), BF16),
            pltpu.VMEM((4, 80, 384), BF16),
            pltpu.VMEM((4, 80, 384), BF16),
            pltpu.VMEM((16, 16, 128), BF16),
            pltpu.VMEM((4, 4, 16, 128), BF16),
            pltpu.VMEM((8, 4, 16, 128), BF16),
            pltpu.VMEM((2, 4, 16, 16, 128), BF16),
            pltpu.VMEM((256, LANES), BF16),
            pltpu.VMEM((NO, 1664), BF16),
            pltpu.VMEM((NO, 1664), F32),
            pltpu.VMEM((4, NO, 512), BF16),
            pltpu.VMEM((4 * PHASES, NO * QP, 128), F32),
            pltpu.VMEM((PHASES, 8, 16, 16, 128), BF16),
            pltpu.VMEM((PHASES, 8, 16, 16, 128), BF16),
            pltpu.VMEM((4, 160, 512), BF16),
            pltpu.VMEM((160, LANES), F32),
            pltpu.VMEM((20, 8, LANES), F32),
            pltpu.VMEM((32, 16, 384), BF16),
            pltpu.VMEM((32, 16, 512), BF16),
            pltpu.VMEM((32, 1, 128), F32),
            pltpu.VMEM((32, 8, 128), F32),
            pltpu.VMEM((CHIPS, 16, 384), BF16),
            pltpu.VMEM((CHIPS, 16, 512), BF16),
            pltpu.VMEM((CHIPS, 1, 128), F32),
            pltpu.VMEM((CHIPS, 128), F32),
            DMA((17,)),
            DMA((4,)), DMA((4,)), DMA((4,)), DMA((4,)),
            DMA((4,)), DMA((4,)), DMA((8,)), DMA((8,)),
            DMA((4,)), DMA((4,)),
            DMA((4, 4)), DMA((4, 4)), DMA((4, 4)), DMA((4, 4)),
            DMA((PHASES, 7)), DMA((PHASES, 8)),
            DMA((3, 32)), DMA((3, CHIPS)),
        ],
        compiler_params=pltpu.CompilerParams(
            collective_id=0, has_side_effects=True, vmem_limit_bytes=53 * 1024 * 1024),
        name="rotate",
    )(three_index, jnp.transpose(density, (0, 2, 1)), hess_diag.T)
    return pairs.T[None]


def solution(mesh):
    return jax.shard_map(
        on_device,
        mesh=mesh,
        in_specs=(P("aux", "orb", None), P("aux", "orb", None), P()),
        out_specs=P("orb", None, "aux"),
        check_vma=False,
    )
```

```python
import functools
import math

import jax
import jax.numpy as jnp
from jax import lax
from jax.experimental import pallas as pl
from jax.experimental.pallas import tpu as pltpu
from jax.sharding import PartitionSpec as P

MESH = pl.DeviceIdType.MESH
F32 = jnp.float32
BF16 = jnp.bfloat16
NT = (((1,), (1,)), ((), ()))

NO = 160
LANES = 1536
CHIPS = 32
TILES = 15
EARLY = (0, 4, 5, 9, 10, 14, 15, 19)
ROW_ORDER = EARLY + tuple(n for n in range(20) if n not in EARLY)
PARTS = ((0, 0, 2, 0), (0, 2, 5, 7), (1, 0, 2, 0), (1, 2, 5, 7))
PHASES = 2
QP = 8 // PHASES

def place():
    aux = lax.axis_index("aux")
    orb = lax.axis_index("orb")
    return aux, orb, lax.rem(aux, 2), lax.div(aux, 2)


def remote(src, dst, send_sem, recv_sem, aux, orb):
    return pltpu.make_async_remote_copy(
        src_ref=src, dst_ref=dst, send_sem=send_sem, recv_sem=recv_sem,
        device_id={"aux": aux, "orb": orb}, device_id_type=MESH,
    )


def kernel(b_hbm, d_hbm, h_hbm, out, bv, dv, hl, hv, acc, cs, cr, xs, xr, ys, yr, zr, g,
           gb, u, left, lx, hs, hb, hr, hx, rot, rc, ob, oc, lo, kept, rv, rw, lr, rest_rows,
           load_sem, cs_sem, cr_sem, xs_sem, xr_sem, ys_sem, yr_sem, zs_sem, zr_sem,
           gs_sem, gr_sem, gxs_sem, gxr_sem, gcs_sem, gcr_sem,
           hs_sem, hr_sem, os_sem, or_sem):
    aux, orb, core, chip = place()
    peer = aux + 1 - 2 * core
    barrier = pltpu.get_barrier_semaphore()

    loads = []
    for q in range(8):
        loads.append((
            pltpu.make_async_copy(d_hbm.at[q], dv.at[q], load_sem.at[2 * q]),
            pltpu.make_async_copy(b_hbm.at[q], bv.at[q], load_sem.at[2 * q + 1]),
        ))
        for copy in loads[-1]:
            copy.start()
    hess_load = pltpu.make_async_copy(h_hbm, hl, load_sem.at[16])
    hess_load.start()

    pl.semaphore_signal(barrier, inc=1, device_id={"aux": peer, "orb": orb}, device_id_type=MESH)
    for step in range(1, 4):
        pl.semaphore_signal(barrier, inc=1, device_id={"aux": aux, "orb": lax.rem(orb + step, 4)},
                            device_id_type=MESH)

    for step in range(1, 4):
        other = lax.rem(lax.div(chip, 8) + step, 4) * 8 + lax.rem(chip, 8)
        pl.semaphore_signal(barrier, inc=1, device_id={"aux": 2 * other + core, "orb": orb}, device_id_type=MESH)
    for step in range(1, 8):
        other = lax.div(chip, 8) * 8 + lax.rem(chip + step, 8)
        pl.semaphore_signal(barrier, inc=1, device_id={"aux": 2 * other + core, "orb": orb}, device_id_type=MESH)

    near = [(0, 1)] + [(step, flip) for step in (2, 1, 3) for flip in (0, 1)]

    def near_device(step, flip):
        other_core = core + flip - 2 * core * flip
        return 2 * chip + other_core, lax.rem(orb + step, 4), other_core

    g[:, :, TILES] = jnp.zeros((2, 4, 16, 128), BF16)
    ys[TILES] = jnp.zeros((16, 128), BF16)
    acc[3, :, 256:384] = jnp.zeros((NO, 128), F32)

    for q in range(8):
        for copy in loads[q]:
            copy.wait()
        part = jnp.dot(dv[q], bv[q, :, 128:1600], preferred_element_type=F32)
        for x in range(4):
            width = 384 if x < 3 else 320
            piece = part[:, 384 * x:384 * x + width]
            if q == 0:
                acc[x, :, :width] = piece
            else:
                acc[x, :, :width] += piece
    hess_load.wait()
    hv[:, 0:1408] = hl[:, 0:1408]
    hv[:, 1408:1536] = jnp.concatenate([hl[:, 1408:1440], jnp.ones((NO, 96), F32)], axis=1)
    pl.semaphore_wait(barrier, 14)

    other_rows = pl.ds(pl.multiple_of(80 * (1 - core), 16), 80)
    my_rows = pl.ds(pl.multiple_of(80 * core, 16), 80)
    core_copies = []
    order = [lax.rem(orb + step, 4) for step in (2, 1, 3, 0)]
    for x in order:
        cs[x] = acc[x, other_rows, :].astype(BF16)
        copy = remote(cs.at[x], cr.at[x], cs_sem.at[x], cr_sem.at[x], peer, orb)
        copy.start()
        core_copies.append(copy)
    x_copies = []
    for n, x in enumerate(order[:3]):
        core_copies[n].wait_recv()
        xs[x] = (acc[x, my_rows, :] + cr[x].astype(F32)).astype(BF16)
        copy = remote(xs.at[x], xr.at[orb], xs_sem.at[x], xr_sem.at[orb], aux, x)
        copy.start()
        x_copies.append(copy)
    core_copies[3].wait_recv()
    total = acc[orb, my_rows, :] + cr[orb].astype(F32)
    for step in range(1, 4):
        src = lax.rem(orb + step, 4)
        remote(xs.at[src], xr.at[src], xs_sem.at[src], xr_sem.at[src], aux, src).wait_recv()
        total = total + xr[src].astype(F32)
    for k in range(5):
        for t in range(3):
            ys[3 * k + t] = total[16 * k:16 * k + 16, 128 * t:128 * t + 128].astype(BF16)

    row, z = lax.div(chip, 8), lax.rem(chip, 8)
    yz_copies = []
    for step in (2, 1, 3):
        other = lax.rem(row + step, 4)
        copy = remote(ys.at[pl.ds(4 * other, 4)], yr.at[row], ys_sem.at[step], yr_sem.at[row],
                      (8 * other + z) * 2 + core, orb)
        copy.start()
        yz_copies.append(copy)
    yr[row] = ys[pl.ds(4 * row, 4)]
    for step in (1, 3, 2):
        src = lax.rem(row + step, 4)
        remote(yr.at[src], yr.at[src], ys_sem.at[0], yr_sem.at[src], aux, orb).wait_recv()
    fock = yr[0].astype(F32)
    for src in range(1, 4):
        fock = fock + yr[src].astype(F32)
    zr[z] = fock.astype(BF16)

    for step in (4, 3, 5, 2, 6, 1, 7):
        far = lax.rem(z + step, 8)
        copy = remote(zr.at[z], zr.at[z], zs_sem.at[step], zr_sem.at[z], (8 * row + far) * 2 + core, orb)
        copy.start()
        yz_copies.append(copy)
    hess = []
    in_tile = lax.broadcasted_iota(jnp.int32, (16, 128), 1)
    for n in range(4):
        tile = jnp.minimum(4 * row + n, TILES - 1)
        lane_tile = orb * 3 + lax.rem(tile, 3)
        hess_rows = pl.ds(pl.multiple_of(80 * core + 16 * lax.div(tile, 3), 16), 16)
        before = hv[hess_rows, pl.ds(pl.multiple_of(jnp.maximum(lane_tile - 1, 0) * 128, 128), 128)]
        after = hv[hess_rows, pl.ds(pl.multiple_of(lane_tile * 128, 128), 128)]
        lane = lane_tile * 128 + in_tile
        valid = jnp.logical_and(lane >= 32, lane < 1472)
        hess.append((valid, pltpu.roll(jnp.where(in_tile < 96, after, before), 32, 1)))
    for step in (1, 7, 2, 6, 3, 5, 4):
        src = lax.rem(z + step, 8)
        remote(zr.at[src], zr.at[src], zs_sem.at[0], zr_sem.at[src], aux, orb).wait_recv()
    for n in range(4):
        fock = zr[0, n].astype(F32)
        for src in range(1, 8):
            fock = fock + zr[src, n].astype(F32)
        valid, tile_hess = hess[n]
        @pl.when(4 * row + n < TILES)
        def _():
            g[core, orb, 4 * row + n] = jnp.where(valid, -fock / tile_hess, 0.0).astype(BF16)

    own = g.at[core, orb, pl.ds(4 * row, 4)]
    for step in (2, 1, 3):
        other = lax.rem(row + step, 4)
        copy = remote(own, own, gs_sem.at[step], gr_sem.at[row], (8 * other + z) * 2 + core, orb)
        copy.start()
        yz_copies.append(copy)
    groups = [lax.rem(row + step, 4) for step in (0, 1, 3, 2)]
    for n, group in enumerate(groups):
        own = g.at[core, orb, pl.ds(4 * group, 4)]
        if n:
            remote(own, own, gs_sem.at[0], gr_sem.at[group], aux, orb).wait_recv()
        for step in (2, 1, 3):
            x = lax.rem(orb + step, 4)
            remote(own, own, gxs_sem.at[x, group], gxr_sem.at[orb, group], aux, x).start()
        remote(own, own, gcs_sem.at[orb, group], gcr_sem.at[orb, group], peer, orb).start()
    for group in groups:
        for step in (1, 3, 2):
            x = lax.rem(orb + step, 4)
            there = g.at[core, x, pl.ds(4 * group, 4)]
            remote(there, there, gxs_sem.at[x, group], gxr_sem.at[x, group], aux, x).wait_recv()
            remote(there, there, gcs_sem.at[x, group], gcr_sem.at[x, group], peer, orb).start()
    for group in groups:
        for step in (0, 1, 3, 2):
            x = lax.rem(orb + step, 4)
            there = g.at[1 - core, x, pl.ds(4 * group, 4)]
            remote(there, there, gcs_sem.at[x, group], gcr_sem.at[x, group], peer, orb).wait_recv()

    for c in range(2):
        for x in range(4):
            for k in range(5):
                for t in range(3):
                    tile = g[c, x, 3 * k + t]
                    lanes = 384 * x + 128 * t
                    gb[80 * c + 16 * k:80 * c + 16 * k + 16, lanes:lanes + 128] = tile
    gb[NO:, :] = jnp.zeros((256 - NO, LANES), BF16)
    gen = gb[0:NO, :].astype(F32)
    norm = jnp.sqrt(jnp.sum(gen * gen, axis=(0, 1), keepdims=True))
    scale = jnp.minimum(1.0, math.sqrt(NO) / norm)
    gram = lax.dot_general(gb[...], gb[...], NT, preferred_element_type=F32)
    inter = gram * (scale * scale)
    inter_b = inter.astype(BF16)
    squared = jnp.dot(inter_b[:NO], inter_b, preferred_element_type=F32)
    over = jnp.dot(inter_b[:NO], gb[...], preferred_element_type=F32) * scale
    rotation = gen * scale
    inter = inter[:NO]
    eye = jnp.where(lax.broadcasted_iota(jnp.int32, (NO, 256), 0)
                    == lax.broadcasted_iota(jnp.int32, (NO, 256), 1), 1.0, 0.0)
    occ = eye - inter / 2.0 + squared / 24.0
    occ_left = inter / 6.0 - eye
    vir = rotation - over / 6.0
    vir_left = over / 24.0 - rotation / 2.0
    early = lax.broadcasted_iota(jnp.int32, (NO, 128), 1) < 32
    u[:, 0:128] = occ[:, 0:128].astype(BF16)
    u[:, 128:256] = jnp.where(early, occ[:, 128:256], vir[:, 0:128]).astype(BF16)
    u[:, 256:1664] = vir[:, 128:1536].astype(BF16)
    to_row = lax.broadcasted_iota(jnp.int32, (NO, NO), 0)
    wanted = jnp.zeros((NO, NO), jnp.int32)
    for n, i in enumerate(ROW_ORDER):
        wanted = jnp.where(to_row % 20 == n, to_row - n + i, wanted)
    order_rows = jnp.where(lax.broadcasted_iota(jnp.int32, (NO, NO), 1) == wanted, 1.0, 0.0).astype(BF16)
    u[...] = jnp.dot(order_rows, u[...], preferred_element_type=F32).astype(BF16)
    left[:, 0:128] = occ_left[:, 0:128]
    left[:, 128:256] = jnp.where(early, occ_left[:, 128:256], vir_left[:, 0:128])
    left[:, 256:1664] = vir_left[:, 128:1536]
    own_lanes = lax.broadcasted_iota(jnp.int32, (NO, 512), 1) < 400
    for x in range(4):
        window = left[:, 384 * x:384 * x + 512]
        if x:
            window = pltpu.roll(window, 512 - 16 * x, 1)
        lx[x] = jnp.where(own_lanes, window, 0.0).astype(BF16)

    pad = jnp.zeros((NO, 112), F32)
    copies = []

    def message(part):
        p, first, last, tile = PARTS[part]
        return p, pl.ds(tile, 3 * (last - first) + 1)

    def send_part(part, n):
        p, tiles = message(part)
        to_aux, to_orb, to_core = near_device(*near[n])
        copy = remote(hb.at[p, 2 * to_orb + to_core, tiles], hr.at[p, 2 * orb + core, tiles], hs_sem.at[part, n],
                      hr_sem.at[part, 2 * orb + core], to_aux, to_orb)
        copy.start()
        copies.append(copy)

    for p in range(PHASES):
        for n in range(QP):
            half = lax.dot_general(u[:, 0:1600], bv[QP * p + n], NT, preferred_element_type=F32)
            half = jnp.concatenate([half, pad], axis=1)
            for t in range(4):
                hs[4 * p + t, pl.ds(n, NO, stride=QP), :] = half[:, 128 * t:128 * t + 128]
        for dest in range(8):
            for _, first_group, last_group, tile in [part for part in PARTS if part[0] == p]:
                tail = None
                for k in range(first_group, last_group):
                    rows = pl.ds(80 * dest + 16 * k, 16)
                    for t in range(3):
                        hb[p, dest, tile + 3 * (k - first_group) + t] = hs[4 * p + t, rows, :].astype(BF16)
                    piece = hs[4 * p + 3, rows, :]
                    tail = piece if tail is None else tail + pltpu.roll(piece, 16 * (k - first_group), 1)
                hb[p, dest, tile + 3 * (last_group - first_group)] = tail.astype(BF16)
        for part in range(4):
            if PARTS[part][0] == p:
                for n in range(7):
                    send_part(part, n)
        hr[p, 2 * orb + core] = hb[p, 2 * orb + core]

    tail_lanes = lax.broadcasted_iota(jnp.int32, (16, 128), 1) < 16
    upper = lax.broadcasted_iota(jnp.int32, (8, 128), 0) < 4
    upper_all = lax.broadcasted_iota(jnp.int32, (8, LANES), 0) < 4
    lane = lax.broadcasted_iota(jnp.int32, (8, 1024), 1)

    def block(d):
        j, first = divmod(900 * d, 1440)
        count = min(900, 1440 - first)
        found = pltpu.roll(rc[j], (LANES - 32 - first) % LANES, 1)[:, :1024]
        if count < 900:
            found = jnp.where(lane < count, found, pltpu.roll(rc[j + 1], (count - 32) % LANES, 1)[:, :1024])
        return found

    def row_of_rest(found, p):
        rest = jnp.where(lane[:, :128] < 4, found[:, 896:1024], 0.0)
        return jnp.sum(pltpu.roll(rest, 32 * p, 1, stride=4, stride_axis=0), axis=0, keepdims=True)

    def send_block(p, d, near_by):
        target = 32 * core + d

        routes = [(ob.at[d], rv.at[chip])] if p == 0 else [(oc.at[d], rw.at[chip]), (lo.at[d], lr.at[chip])]

        def go():
            for n, (src, dst) in enumerate(routes):
                remote(src, dst, os_sem.at[p + n, d], or_sem.at[p + n, chip], target, orb).start()
        if near_by:
            pl.when(target != aux)(go)
            @pl.when(target == aux)
            def _():
                for n, (src, dst) in enumerate(routes):
                    pltpu.make_async_copy(src, dst, or_sem.at[p + n, chip]).start()
        else:
            go()

    for part, (p, first_group, last_group, tile) in enumerate(PARTS):
        _, tiles = message(part)
        for step, flip in near:
            _, from_orb, from_core = near_device(step, flip)
            there = hr.at[p, 2 * from_orb + from_core, tiles]
            remote(there, there, hs_sem.at[part, 0], hr_sem.at[part, 2 * from_orb + from_core], aux, orb).wait_recv()
        count = 16 * (last_group - first_group)
        for x in range(4):
            for c in range(2):
                tail = hr[p, 2 * x + c, tile + 3 * (last_group - first_group)].astype(F32)
                for k in range(last_group - first_group):
                    rows = pl.ds(count * c + 16 * k, 16)
                    for t in range(3):
                        hx[x, rows, 128 * t:128 * t + 128] = hr[p, 2 * x + c, tile + 3 * k + t]
                    piece = pltpu.roll(tail, 128 - 16 * k, 1) if k else tail
                    hx[x, rows, 384:512] = jnp.where(tail_lanes, piece, 0.0).astype(BF16)
        both = pl.ds(0, 2 * count)
        mid = lax.dot_general(hx[0, both], lx[0], NT, preferred_element_type=F32)
        for x in range(1, 4):
            mid = mid + lax.dot_general(hx[x, both], lx[x], NT, preferred_element_type=F32)
        rot[both, :] = jnp.dot((mid * scale).astype(BF16), gb[0:NO, :], preferred_element_type=F32)
        rot[both, 0:384] += hx[0, both, 128:512].astype(F32)
        for x, lanes in ((1, 256), (2, 640), (3, 1024)):
            rot[both, lanes:lanes + 512] += pltpu.roll(hx[x, both].astype(F32), 16 * x, 1)
        for m in range(count // 8):
            first_core = rot[8 * m:8 * m + 8, :]
            second_core = rot[count + 8 * m:count + 8 * m + 8, :]
            at = 4 * first_group + 2 * m
            rc[ROW_ORDER[at]] = jnp.where(upper_all, first_core, pltpu.roll(second_core, 4, 0))
            rc[ROW_ORDER[at + 1]] = jnp.where(upper_all, pltpu.roll(first_core, 4, 0), second_core)
        for d in range(32):
            if (d % 8 in (0, 7)) != (first_group == 0):
                continue
            found = block(d)
            if p == 0:
                ob[d] = jnp.concatenate([found[:, 0:384], found[:, 384:768]], axis=0).astype(BF16)
                kept[d] = found[:, 768:896]
                lo[d] = row_of_rest(found, 0)
            else:
                second = jnp.concatenate([found[:, 512:896], kept[d]], axis=1)
                oc[d] = jnp.concatenate([found[:, 0:512], second], axis=0).astype(BF16)
                lo[d] += row_of_rest(found, 1)
        if first_group == 0:
            for k in range(4):
                turn = lax.rem(lax.div(z, 2) + k, 4)
                for half_y in range(2):
                    send_block(p, 16 * half_y + 8 * lax.div(turn, 2) + 7 * lax.rem(turn, 2), True)
            continue
        for step_z in (4, 3, 5, 2, 6, 1, 7, 0):
            for half_y in range(2):
                for to_core in range(2):
                    d = 16 * half_y + 2 * lax.rem(z + step_z, 8) + to_core
                    whole = lax.rem(d, 8)
                    @pl.when(jnp.logical_and(whole != 0, whole != 7))
                    def _():
                        send_block(p, d, step_z == 0)

    def lay_out(k, carry):
        group = lax.rem(row + k, 4)

        def land(n, inner):
            src = 8 * group + n
            for n, (block_of, there) in enumerate(((ob, rv), (oc, rw), (lo, lr))):
                pltpu.make_async_copy(block_of.at[0], there.at[src], or_sem.at[n, src]).wait()
            rest_rows[pl.ds(src, 1), :] = lr[src]
            return inner
        lax.fori_loop(0, 8, land, 0)
        lanes = pl.ds(pl.multiple_of(128 * group, 128), 128)
        for t in range(7):
            found = []
            for n in range(8):
                src = 8 * group + n
                if t < 3:
                    early = rv[src, :, 128 * t:128 * t + 128].astype(F32)[0:8]
                elif t < 6:
                    early = rv[src, :, 128 * t - 384:128 * t - 256].astype(F32)[8:16]
                else:
                    early = rw[src, :, 384:512].astype(F32)[8:16]
                if t < 4:
                    late = rw[src, :, 128 * t:128 * t + 128].astype(F32)[0:8]
                else:
                    late = rw[src, :, 128 * t - 512:128 * t - 384].astype(F32)[8:16]
                found.append(jnp.where(upper, early, pltpu.roll(late, 4, 0)))
                found.append(jnp.where(upper, pltpu.roll(early, 4, 0), late))
            out[128 * t:128 * t + 128, lanes] = jnp.concatenate(found, axis=0).T.astype(BF16)
        return carry
    lax.fori_loop(0, 4, lay_out, 0)

    at, turn = lax.broadcasted_iota(jnp.int32, (512, 128), 0), lax.broadcasted_iota(jnp.int32, (512, 128), 1)
    chips = lax.broadcasted_iota(jnp.int32, (512, 32), 1)
    spread = jnp.where(lax.broadcasted_iota(jnp.int32, (512, 32), 0) // 16 == chips, 1.0, 0.0).astype(BF16)
    wide = jnp.dot(spread, rest_rows[...].astype(BF16), preferred_element_type=F32)
    wanted = 8 * (at // 4 % 2) + 4 * (at // 8 % 2) + at % 4
    wide = jnp.where(turn // 4 == wanted, wide, 0.0).astype(BF16)
    column = lax.broadcasted_iota(jnp.int32, (16, 128), 0)
    pick = jnp.where(lax.broadcasted_iota(jnp.int32, (16, 128), 1) % 4 == column, 1.0, 0.0).astype(BF16)
    rest = lax.dot_general(pick, wide, NT, preferred_element_type=F32)
    out[896:900, :] = rest[0:4].astype(BF16)

    for copy in core_copies + x_copies + yz_copies:
        copy.wait_send()
    for x in range(4):
        for group in range(4):
            there = g.at[core, x, pl.ds(4 * group, 4)]
            remote(there, there, gcs_sem.at[x, group], gcr_sem.at[x, group], peer, orb).wait_send()
        @pl.when(orb != x)
        def _():
            for group in range(4):
                own = g.at[core, orb, pl.ds(4 * group, 4)]
                remote(own, own, gxs_sem.at[x, group], gxr_sem.at[orb, group], aux, x).wait_send()

    def sent_block(d, carry):
        target = 32 * core + d
        @pl.when(target != aux)
        def _():
            for n, (src, dst) in enumerate(((ob, rv), (oc, rw), (lo, lr))):
                remote(src.at[d], dst.at[chip], os_sem.at[n, d], or_sem.at[n, chip], target, orb).wait_send()
        return carry
    lax.fori_loop(0, 32, sent_block, 0)
    for copy in copies:
        copy.wait_send()


DMA = pltpu.SemaphoreType.DMA
ANY = pl.BlockSpec(memory_space=pl.ANY)
VM = pl.BlockSpec(memory_space=pltpu.VMEM)


def on_device(three_index, density, hess_diag):
    pairs = pl.pallas_call(
        kernel,
        out_shape=jax.ShapeDtypeStruct((900, 512), BF16),
        in_specs=[ANY, ANY, ANY],
        out_specs=VM,
        scratch_shapes=[
            pltpu.VMEM((8, 400, 1600), BF16),
            pltpu.VMEM((8, NO, 400), BF16),
            pltpu.VMEM((NO, 1440), F32),
            pltpu.VMEM((NO, LANES), F32),
            pltpu.VMEM((4, NO, 384), F32),
            pltpu.VMEM((4, 80, 384), BF16),
            pltpu.VMEM((4, 80, 384), BF16),
            pltpu.VMEM((4, 80, 384), BF16),
            pltpu.VMEM((4, 80, 384), BF16),
            pltpu.VMEM((16, 16, 128), BF16),
            pltpu.VMEM((4, 4, 16, 128), BF16),
            pltpu.VMEM((8, 4, 16, 128), BF16),
            pltpu.VMEM((2, 4, 16, 16, 128), BF16),
            pltpu.VMEM((256, LANES), BF16),
            pltpu.VMEM((NO, 1664), BF16),
            pltpu.VMEM((NO, 1664), F32),
            pltpu.VMEM((4, NO, 512), BF16),
            pltpu.VMEM((4 * PHASES, NO * QP, 128), F32),
            pltpu.VMEM((PHASES, 8, 17, 16, 128), BF16),
            pltpu.VMEM((PHASES, 8, 17, 16, 128), BF16),
            pltpu.VMEM((4, 160, 512), BF16),
            pltpu.VMEM((160, LANES), F32),
            pltpu.VMEM((20, 8, LANES), F32),
            pltpu.VMEM((32, 16, 384), BF16),
            pltpu.VMEM((32, 16, 512), BF16),
            pltpu.VMEM((32, 1, 128), F32),
            pltpu.VMEM((32, 8, 128), F32),
            pltpu.VMEM((CHIPS, 16, 384), BF16),
            pltpu.VMEM((CHIPS, 16, 512), BF16),
            pltpu.VMEM((CHIPS, 1, 128), F32),
            pltpu.VMEM((CHIPS, 128), F32),
            DMA((17,)),
            DMA((4,)), DMA((4,)), DMA((4,)), DMA((4,)),
            DMA((4,)), DMA((4,)), DMA((8,)), DMA((8,)),
            DMA((4,)), DMA((4,)),
            DMA((4, 4)), DMA((4, 4)), DMA((4, 4)), DMA((4, 4)),
            DMA((4, 7)), DMA((4, 8)),
            DMA((3, 32)), DMA((3, CHIPS)),
        ],
        compiler_params=pltpu.CompilerParams(
            collective_id=0, has_side_effects=True, vmem_limit_bytes=53 * 1024 * 1024),
        name="rotate",
    )(three_index, jnp.transpose(density, (0, 2, 1)), hess_diag.T)
    return pairs.T[None]


def solution(mesh):
    return jax.shard_map(
        on_device,
        mesh=mesh,
        in_specs=(P("aux", "orb", None), P("aux", "orb", None), P()),
        out_specs=P("orb", None, "aux"),
        check_vma=False,
    )
```

```python
import functools
import math

import jax
import jax.numpy as jnp
from jax import lax
from jax.experimental import pallas as pl
from jax.experimental.pallas import tpu as pltpu
from jax.sharding import PartitionSpec as P

MESH = pl.DeviceIdType.MESH
F32 = jnp.float32
BF16 = jnp.bfloat16
NT = (((1,), (1,)), ((), ()))

NO = 160
LANES = 1536
CHIPS = 32
TILES = 15
EARLY = (0, 4, 5, 9, 10, 14, 15, 19)
ROW_ORDER = EARLY + tuple(n for n in range(20) if n not in EARLY)
PARTS = ((0, 0, 2, 0), (0, 2, 5, 7), (1, 0, 2, 0), (1, 2, 5, 7))
PHASES = 2
QP = 8 // PHASES

def place():
    aux = lax.axis_index("aux")
    orb = lax.axis_index("orb")
    return aux, orb, lax.rem(aux, 2), lax.div(aux, 2)


def remote(src, dst, send_sem, recv_sem, aux, orb):
    return pltpu.make_async_remote_copy(
        src_ref=src, dst_ref=dst, send_sem=send_sem, recv_sem=recv_sem,
        device_id={"aux": aux, "orb": orb}, device_id_type=MESH,
    )


def kernel(b_hbm, d_hbm, h_hbm, out, bv, dv, hl, hv, acc, cs, cr, xs, xr, ys, yr, zr, g,
           gb, u, left, lx, hs, hb, hr, hx, rot, rc, ob, oc, lo, kept, rv, rw, lr, rest_rows,
           load_sem, cs_sem, cr_sem, xs_sem, xr_sem, ys_sem, yr_sem, zs_sem, zr_sem,
           gs_sem, gr_sem, gxs_sem, gxr_sem, gcs_sem, gcr_sem,
           hs_sem, hr_sem, os_sem, or_sem):
    aux, orb, core, chip = place()
    peer = aux + 1 - 2 * core
    barrier = pltpu.get_barrier_semaphore()

    loads = []
    for q in range(8):
        loads.append((
            pltpu.make_async_copy(d_hbm.at[q], dv.at[q], load_sem.at[2 * q]),
            pltpu.make_async_copy(b_hbm.at[q], bv.at[q], load_sem.at[2 * q + 1]),
        ))
        for copy in loads[-1]:
            copy.start()
    hess_load = pltpu.make_async_copy(h_hbm, hl, load_sem.at[16])
    hess_load.start()

    pl.semaphore_signal(barrier, inc=1, device_id={"aux": peer, "orb": orb}, device_id_type=MESH)
    for step in range(1, 4):
        pl.semaphore_signal(barrier, inc=1, device_id={"aux": aux, "orb": lax.rem(orb + step, 4)},
                            device_id_type=MESH)

    for step in range(1, 4):
        other = lax.rem(lax.div(chip, 8) + step, 4) * 8 + lax.rem(chip, 8)
        pl.semaphore_signal(barrier, inc=1, device_id={"aux": 2 * other + core, "orb": orb}, device_id_type=MESH)
    for step in range(1, 8):
        other = lax.div(chip, 8) * 8 + lax.rem(chip + step, 8)
        pl.semaphore_signal(barrier, inc=1, device_id={"aux": 2 * other + core, "orb": orb}, device_id_type=MESH)

    near = [(0, 1)] + [(step, flip) for step in (2, 1, 3) for flip in (0, 1)]

    def near_device(step, flip):
        other_core = core + flip - 2 * core * flip
        return 2 * chip + other_core, lax.rem(orb + step, 4), other_core

    g[:, :, TILES] = jnp.zeros((2, 4, 16, 128), BF16)
    ys[TILES] = jnp.zeros((16, 128), BF16)
    acc[3, :, 256:384] = jnp.zeros((NO, 128), F32)

    for q in range(8):
        for copy in loads[q]:
            copy.wait()
        part = jnp.dot(dv[q], bv[q, :, 128:1600], preferred_element_type=F32)
        for x in range(4):
            width = 384 if x < 3 else 320
            piece = part[:, 384 * x:384 * x + width]
            if q == 0:
                acc[x, :, :width] = piece
            else:
                acc[x, :, :width] += piece
    hess_load.wait()
    hv[:, 0:1408] = hl[:, 0:1408]
    hv[:, 1408:1536] = jnp.concatenate([hl[:, 1408:1440], jnp.ones((NO, 96), F32)], axis=1)
    pl.semaphore_wait(barrier, 14)

    other_rows = pl.ds(pl.multiple_of(80 * (1 - core), 16), 80)
    my_rows = pl.ds(pl.multiple_of(80 * core, 16), 80)
    core_copies = []
    order = [lax.rem(orb + step, 4) for step in (2, 1, 3, 0)]
    for x in order:
        cs[x] = acc[x, other_rows, :].astype(BF16)
        copy = remote(cs.at[x], cr.at[x], cs_sem.at[x], cr_sem.at[x], peer, orb)
        copy.start()
        core_copies.append(copy)
    x_copies = []
    for n, x in enumerate(order[:3]):
        core_copies[n].wait_recv()
        xs[x] = (acc[x, my_rows, :] + cr[x].astype(F32)).astype(BF16)
        copy = remote(xs.at[x], xr.at[orb], xs_sem.at[x], xr_sem.at[orb], aux, x)
        copy.start()
        x_copies.append(copy)
    core_copies[3].wait_recv()
    total = acc[orb, my_rows, :] + cr[orb].astype(F32)
    for step in range(1, 4):
        src = lax.rem(orb + step, 4)
        remote(xs.at[src], xr.at[src], xs_sem.at[src], xr_sem.at[src], aux, src).wait_recv()
        total = total + xr[src].astype(F32)
    for k in range(5):
        for t in range(3):
            ys[3 * k + t] = total[16 * k:16 * k + 16, 128 * t:128 * t + 128].astype(BF16)

    row, z = lax.div(chip, 8), lax.rem(chip, 8)
    yz_copies = []
    for step in (2, 1, 3):
        other = lax.rem(row + step, 4)
        copy = remote(ys.at[pl.ds(4 * other, 4)], yr.at[row], ys_sem.at[step], yr_sem.at[row],
                      (8 * other + z) * 2 + core, orb)
        copy.start()
        yz_copies.append(copy)
    yr[row] = ys[pl.ds(4 * row, 4)]
    for step in (1, 3, 2):
        src = lax.rem(row + step, 4)
        remote(yr.at[src], yr.at[src], ys_sem.at[0], yr_sem.at[src], aux, orb).wait_recv()
    fock = yr[0].astype(F32)
    for src in range(1, 4):
        fock = fock + yr[src].astype(F32)
    zr[z] = fock.astype(BF16)

    for step in (4, 3, 5, 2, 6, 1, 7):
        far = lax.rem(z + step, 8)
        copy = remote(zr.at[z], zr.at[z], zs_sem.at[step], zr_sem.at[z], (8 * row + far) * 2 + core, orb)
        copy.start()
        yz_copies.append(copy)
    hess = []
    in_tile = lax.broadcasted_iota(jnp.int32, (16, 128), 1)
    for n in range(4):
        tile = jnp.minimum(4 * row + n, TILES - 1)
        lane_tile = orb * 3 + lax.rem(tile, 3)
        hess_rows = pl.ds(pl.multiple_of(80 * core + 16 * lax.div(tile, 3), 16), 16)
        before = hv[hess_rows, pl.ds(pl.multiple_of(jnp.maximum(lane_tile - 1, 0) * 128, 128), 128)]
        after = hv[hess_rows, pl.ds(pl.multiple_of(lane_tile * 128, 128), 128)]
        lane = lane_tile * 128 + in_tile
        valid = jnp.logical_and(lane >= 32, lane < 1472)
        hess.append((valid, pltpu.roll(jnp.where(in_tile < 96, after, before), 32, 1)))
    for step in (1, 7, 2, 6, 3, 5, 4):
        src = lax.rem(z + step, 8)
        remote(zr.at[src], zr.at[src], zs_sem.at[0], zr_sem.at[src], aux, orb).wait_recv()
    for n in range(4):
        fock = zr[0, n].astype(F32)
        for src in range(1, 8):
            fock = fock + zr[src, n].astype(F32)
        valid, tile_hess = hess[n]
        @pl.when(4 * row + n < TILES)
        def _():
            g[core, orb, 4 * row + n] = jnp.where(valid, -fock / tile_hess, 0.0).astype(BF16)

    own = g.at[core, orb, pl.ds(4 * row, 4)]
    for step in (2, 1, 3):
        other = lax.rem(row + step, 4)
        copy = remote(own, own, gs_sem.at[step], gr_sem.at[row], (8 * other + z) * 2 + core, orb)
        copy.start()
        yz_copies.append(copy)
    groups = [lax.rem(row + step, 4) for step in (0, 1, 3, 2)]
    for n, group in enumerate(groups):
        own = g.at[core, orb, pl.ds(4 * group, 4)]
        if n:
            remote(own, own, gs_sem.at[0], gr_sem.at[group], aux, orb).wait_recv()
        for step in (2, 1, 3):
            x = lax.rem(orb + step, 4)
            remote(own, own, gxs_sem.at[x, group], gxr_sem.at[orb, group], aux, x).start()
        remote(own, own, gcs_sem.at[orb, group], gcr_sem.at[orb, group], peer, orb).start()
    for group in groups:
        for step in (1, 3, 2):
            x = lax.rem(orb + step, 4)
            there = g.at[core, x, pl.ds(4 * group, 4)]
            remote(there, there, gxs_sem.at[x, group], gxr_sem.at[x, group], aux, x).wait_recv()
            remote(there, there, gcs_sem.at[x, group], gcr_sem.at[x, group], peer, orb).start()
    for group in groups:
        for step in (0, 1, 3, 2):
            x = lax.rem(orb + step, 4)
            there = g.at[1 - core, x, pl.ds(4 * group, 4)]
            remote(there, there, gcs_sem.at[x, group], gcr_sem.at[x, group], peer, orb).wait_recv()

    for c in range(2):
        for x in range(4):
            for k in range(5):
                for t in range(3):
                    tile = g[c, x, 3 * k + t]
                    lanes = 384 * x + 128 * t
                    gb[80 * c + 16 * k:80 * c + 16 * k + 16, lanes:lanes + 128] = tile
    gb[NO:, :] = jnp.zeros((256 - NO, LANES), BF16)
    gen = gb[0:NO, :].astype(F32)
    norm = jnp.sqrt(jnp.sum(gen * gen, axis=(0, 1), keepdims=True))
    scale = jnp.minimum(1.0, math.sqrt(NO) / norm)
    gram = lax.dot_general(gb[...], gb[...], NT, preferred_element_type=F32)
    inter = gram * (scale * scale)
    inter_b = inter.astype(BF16)
    squared = jnp.dot(inter_b[:NO], inter_b, preferred_element_type=F32)
    over = jnp.dot(inter_b[:NO], gb[...], preferred_element_type=F32) * scale
    rotation = gen * scale
    inter = inter[:NO]
    eye = jnp.where(lax.broadcasted_iota(jnp.int32, (NO, 256), 0)
                    == lax.broadcasted_iota(jnp.int32, (NO, 256), 1), 1.0, 0.0)
    occ = eye - inter / 2.0 + squared / 24.0
    occ_left = inter / 6.0 - eye
    vir = rotation - over / 6.0
    vir_left = over / 24.0 - rotation / 2.0
    early = lax.broadcasted_iota(jnp.int32, (NO, 128), 1) < 32
    u[:, 0:128] = occ[:, 0:128].astype(BF16)
    u[:, 128:256] = jnp.where(early, occ[:, 128:256], vir[:, 0:128]).astype(BF16)
    u[:, 256:1664] = vir[:, 128:1536].astype(BF16)
    to_row = lax.broadcasted_iota(jnp.int32, (NO, NO), 0)
    wanted = jnp.zeros((NO, NO), jnp.int32)
    for n, i in enumerate(ROW_ORDER):
        wanted = jnp.where(to_row % 20 == n, to_row - n + i, wanted)
    order_rows = jnp.where(lax.broadcasted_iota(jnp.int32, (NO, NO), 1) == wanted, 1.0, 0.0).astype(BF16)
    u[...] = jnp.dot(order_rows, u[...], preferred_element_type=F32).astype(BF16)
    left[:, 0:128] = occ_left[:, 0:128]
    left[:, 128:256] = jnp.where(early, occ_left[:, 128:256], vir_left[:, 0:128])
    left[:, 256:1664] = vir_left[:, 128:1536]
    own_lanes = lax.broadcasted_iota(jnp.int32, (NO, 512), 1) < 400
    for x in range(4):
        window = left[:, 384 * x:384 * x + 512]
        if x:
            window = pltpu.roll(window, 512 - 16 * x, 1)
        lx[x] = jnp.where(own_lanes, window, 0.0).astype(BF16)

    pad = jnp.zeros((NO, 112), F32)
    copies = []

    def message(part):
        p, first, last, tile = PARTS[part]
        return p, pl.ds(tile, 3 * (last - first) + 1)

    def send_part(part, n):
        p, tiles = message(part)
        to_aux, to_orb, to_core = near_device(*near[n])
        copy = remote(hb.at[p, 2 * to_orb + to_core, tiles], hr.at[p, 2 * orb + core, tiles], hs_sem.at[part, n],
                      hr_sem.at[part, 2 * orb + core], to_aux, to_orb)
        copy.start()
        copies.append(copy)

    for p in range(PHASES):
        for n in range(QP):
            half = lax.dot_general(u[:, 0:1600], bv[QP * p + n], NT, preferred_element_type=F32)
            half = jnp.concatenate([half, pad], axis=1)
            for t in range(4):
                hs[4 * p + t, pl.ds(n, NO, stride=QP), :] = half[:, 128 * t:128 * t + 128]
        for part, (half_of, first_group, last_group, tile) in enumerate(PARTS):
            if half_of != p:
                continue
            for dest in range(8):
                tail = None
                for k in range(first_group, last_group):
                    rows = pl.ds(80 * dest + 16 * k, 16)
                    for t in range(3):
                        hb[p, dest, tile + 3 * (k - first_group) + t] = hs[4 * p + t, rows, :].astype(BF16)
                    piece = hs[4 * p + 3, rows, :]
                    tail = piece if tail is None else tail + pltpu.roll(piece, 16 * (k - first_group), 1)
                hb[p, dest, tile + 3 * (last_group - first_group)] = tail.astype(BF16)
            for n in range(7):
                send_part(part, n)
        hr[p, 2 * orb + core] = hb[p, 2 * orb + core]

    tail_lanes = lax.broadcasted_iota(jnp.int32, (16, 128), 1) < 16
    upper = lax.broadcasted_iota(jnp.int32, (8, 128), 0) < 4
    upper_all = lax.broadcasted_iota(jnp.int32, (8, LANES), 0) < 4
    lane = lax.broadcasted_iota(jnp.int32, (8, 1024), 1)

    def block(d):
        j, first = divmod(900 * d, 1440)
        count = min(900, 1440 - first)
        found = pltpu.roll(rc[j], (LANES - 32 - first) % LANES, 1)[:, :1024]
        if count < 900:
            found = jnp.where(lane < count, found, pltpu.roll(rc[j + 1], (count - 32) % LANES, 1)[:, :1024])
        return found

    def row_of_rest(found, p):
        rest = jnp.where(lane[:, :128] < 4, found[:, 896:1024], 0.0)
        return jnp.sum(pltpu.roll(rest, 32 * p, 1, stride=4, stride_axis=0), axis=0, keepdims=True)

    def send_block(kind, d, near_by):
        target = 32 * core + d
        source, landing = ((ob, rv), (oc, rw), (lo, lr))[kind]

        def go():
            remote(source.at[d], landing.at[chip], os_sem.at[kind, d], or_sem.at[kind, chip], target, orb).start()
        if near_by:
            pl.when(target != aux)(go)
            @pl.when(target == aux)
            def _():
                pltpu.make_async_copy(source.at[d], landing.at[chip], or_sem.at[kind, chip]).start()
        else:
            go()

    for part, (p, first_group, last_group, tile) in enumerate(PARTS):
        _, tiles = message(part)
        for step, flip in near:
            _, from_orb, from_core = near_device(step, flip)
            there = hr.at[p, 2 * from_orb + from_core, tiles]
            remote(there, there, hs_sem.at[part, 0], hr_sem.at[part, 2 * from_orb + from_core], aux, orb).wait_recv()
        count = 16 * (last_group - first_group)
        for x in range(4):
            for c in range(2):
                tail = hr[p, 2 * x + c, tile + 3 * (last_group - first_group)].astype(F32)
                for k in range(last_group - first_group):
                    rows = pl.ds(count * c + 16 * k, 16)
                    for t in range(3):
                        hx[x, rows, 128 * t:128 * t + 128] = hr[p, 2 * x + c, tile + 3 * k + t]
                    piece = pltpu.roll(tail, 128 - 16 * k, 1) if k else tail
                    hx[x, rows, 384:512] = jnp.where(tail_lanes, piece, 0.0).astype(BF16)
        both = pl.ds(0, 2 * count)
        mid = lax.dot_general(hx[0, both], lx[0], NT, preferred_element_type=F32)
        for x in range(1, 4):
            mid = mid + lax.dot_general(hx[x, both], lx[x], NT, preferred_element_type=F32)
        rot[both, :] = jnp.dot((mid * scale).astype(BF16), gb[0:NO, :], preferred_element_type=F32)
        rot[both, 0:384] += hx[0, both, 128:512].astype(F32)
        for x, lanes in ((1, 256), (2, 640), (3, 1024)):
            rot[both, lanes:lanes + 512] += pltpu.roll(hx[x, both].astype(F32), 16 * x, 1)
        for m in range(count // 8):
            first_core = rot[8 * m:8 * m + 8, :]
            second_core = rot[count + 8 * m:count + 8 * m + 8, :]
            at = 4 * first_group + 2 * m
            rc[ROW_ORDER[at]] = jnp.where(upper_all, first_core, pltpu.roll(second_core, 4, 0))
            rc[ROW_ORDER[at + 1]] = jnp.where(upper_all, pltpu.roll(first_core, 4, 0), second_core)
        for d in range(32):
            if (d % 8 in (0, 7)) != (first_group == 0):
                continue
            found = block(d)
            if p == 0:
                ob[d] = jnp.concatenate([found[:, 0:384], found[:, 384:768]], axis=0).astype(BF16)
                kept[d] = found[:, 768:896]
                lo[d] = row_of_rest(found, 0)
            else:
                second = jnp.concatenate([found[:, 512:896], kept[d]], axis=1)
                oc[d] = jnp.concatenate([found[:, 0:512], second], axis=0).astype(BF16)
                lo[d] += row_of_rest(found, 1)
        if first_group == 0:
            for k in range(4):
                turn = lax.rem(lax.div(z, 2) + k, 4)
                for half_y in range(2):
                    send_block(p, 16 * half_y + 8 * lax.div(turn, 2) + 7 * lax.rem(turn, 2), True)
            continue
        for step_z in (4, 3, 5, 2, 6, 1, 7, 0):
            for half_y in range(2):
                for to_core in range(2):
                    d = 16 * half_y + 2 * lax.rem(z + step_z, 8) + to_core
                    whole = lax.rem(d, 8)
                    @pl.when(jnp.logical_and(whole != 0, whole != 7))
                    def _():
                        send_block(p, d, step_z == 0)

    for step_z in (4, 3, 5, 2, 6, 1, 7, 0):
        for half_y in range(2):
            for to_core in range(2):
                send_block(2, 16 * half_y + 2 * lax.rem(z + step_z, 8) + to_core, step_z == 0)

    def lay_out(k, carry):
        group = lax.rem(row + k, 4)

        def land(n, inner):
            src = 8 * group + n
            for n, (block_of, there) in enumerate(((ob, rv), (oc, rw), (lo, lr))):
                pltpu.make_async_copy(block_of.at[0], there.at[src], or_sem.at[n, src]).wait()
            rest_rows[pl.ds(src, 1), :] = lr[src]
            return inner
        lax.fori_loop(0, 8, land, 0)
        lanes = pl.ds(pl.multiple_of(128 * group, 128), 128)
        for t in range(7):
            found = []
            for n in range(8):
                src = 8 * group + n
                if t < 3:
                    early = rv[src, :, 128 * t:128 * t + 128].astype(F32)[0:8]
                elif t < 6:
                    early = rv[src, :, 128 * t - 384:128 * t - 256].astype(F32)[8:16]
                else:
                    early = rw[src, :, 384:512].astype(F32)[8:16]
                if t < 4:
                    late = rw[src, :, 128 * t:128 * t + 128].astype(F32)[0:8]
                else:
                    late = rw[src, :, 128 * t - 512:128 * t - 384].astype(F32)[8:16]
                found.append(jnp.where(upper, early, pltpu.roll(late, 4, 0)))
                found.append(jnp.where(upper, pltpu.roll(early, 4, 0), late))
            out[128 * t:128 * t + 128, lanes] = jnp.concatenate(found, axis=0).T.astype(BF16)
        return carry
    lax.fori_loop(0, 4, lay_out, 0)

    at, turn = lax.broadcasted_iota(jnp.int32, (512, 128), 0), lax.broadcasted_iota(jnp.int32, (512, 128), 1)
    chips = lax.broadcasted_iota(jnp.int32, (512, 32), 1)
    spread = jnp.where(lax.broadcasted_iota(jnp.int32, (512, 32), 0) // 16 == chips, 1.0, 0.0).astype(BF16)
    wide = jnp.dot(spread, rest_rows[...].astype(BF16), preferred_element_type=F32)
    wanted = 8 * (at // 4 % 2) + 4 * (at // 8 % 2) + at % 4
    wide = jnp.where(turn // 4 == wanted, wide, 0.0).astype(BF16)
    column = lax.broadcasted_iota(jnp.int32, (16, 128), 0)
    pick = jnp.where(lax.broadcasted_iota(jnp.int32, (16, 128), 1) % 4 == column, 1.0, 0.0).astype(BF16)
    rest = lax.dot_general(pick, wide, NT, preferred_element_type=F32)
    out[896:900, :] = rest[0:4].astype(BF16)

    for copy in core_copies + x_copies + yz_copies:
        copy.wait_send()
    for x in range(4):
        for group in range(4):
            there = g.at[core, x, pl.ds(4 * group, 4)]
            remote(there, there, gcs_sem.at[x, group], gcr_sem.at[x, group], peer, orb).wait_send()
        @pl.when(orb != x)
        def _():
            for group in range(4):
                own = g.at[core, orb, pl.ds(4 * group, 4)]
                remote(own, own, gxs_sem.at[x, group], gxr_sem.at[orb, group], aux, x).wait_send()

    def sent_block(d, carry):
        target = 32 * core + d
        @pl.when(target != aux)
        def _():
            for n, (src, dst) in enumerate(((ob, rv), (oc, rw), (lo, lr))):
                remote(src.at[d], dst.at[chip], os_sem.at[n, d], or_sem.at[n, chip], target, orb).wait_send()
        return carry
    lax.fori_loop(0, 32, sent_block, 0)
    for copy in copies:
        copy.wait_send()


DMA = pltpu.SemaphoreType.DMA
ANY = pl.BlockSpec(memory_space=pl.ANY)
VM = pl.BlockSpec(memory_space=pltpu.VMEM)


def on_device(three_index, density, hess_diag):
    pairs = pl.pallas_call(
        kernel,
        out_shape=jax.ShapeDtypeStruct((900, 512), BF16),
        in_specs=[ANY, ANY, ANY],
        out_specs=VM,
        scratch_shapes=[
            pltpu.VMEM((8, 400, 1600), BF16),
            pltpu.VMEM((8, NO, 400), BF16),
            pltpu.VMEM((NO, 1440), F32),
            pltpu.VMEM((NO, LANES), F32),
            pltpu.VMEM((4, NO, 384), F32),
            pltpu.VMEM((4, 80, 384), BF16),
            pltpu.VMEM((4, 80, 384), BF16),
            pltpu.VMEM((4, 80, 384), BF16),
            pltpu.VMEM((4, 80, 384), BF16),
            pltpu.VMEM((16, 16, 128), BF16),
            pltpu.VMEM((4, 4, 16, 128), BF16),
            pltpu.VMEM((8, 4, 16, 128), BF16),
            pltpu.VMEM((2, 4, 16, 16, 128), BF16),
            pltpu.VMEM((256, LANES), BF16),
            pltpu.VMEM((NO, 1664), BF16),
            pltpu.VMEM((NO, 1664), F32),
            pltpu.VMEM((4, NO, 512), BF16),
            pltpu.VMEM((4 * PHASES, NO * QP, 128), F32),
            pltpu.VMEM((PHASES, 8, 17, 16, 128), BF16),
            pltpu.VMEM((PHASES, 8, 17, 16, 128), BF16),
            pltpu.VMEM((4, 160, 512), BF16),
            pltpu.VMEM((160, LANES), F32),
            pltpu.VMEM((20, 8, LANES), F32),
            pltpu.VMEM((32, 16, 384), BF16),
            pltpu.VMEM((32, 16, 512), BF16),
            pltpu.VMEM((32, 1, 128), F32),
            pltpu.VMEM((32, 8, 128), F32),
            pltpu.VMEM((CHIPS, 16, 384), BF16),
            pltpu.VMEM((CHIPS, 16, 512), BF16),
            pltpu.VMEM((CHIPS, 1, 128), F32),
            pltpu.VMEM((CHIPS, 128), F32),
            DMA((17,)),
            DMA((4,)), DMA((4,)), DMA((4,)), DMA((4,)),
            DMA((4,)), DMA((4,)), DMA((8,)), DMA((8,)),
            DMA((4,)), DMA((4,)),
            DMA((4, 4)), DMA((4, 4)), DMA((4, 4)), DMA((4, 4)),
            DMA((4, 7)), DMA((4, 8)),
            DMA((3, 32)), DMA((3, CHIPS)),
        ],
        compiler_params=pltpu.CompilerParams(
            collective_id=0, has_side_effects=True, vmem_limit_bytes=53 * 1024 * 1024),
        name="rotate",
    )(three_index, jnp.transpose(density, (0, 2, 1)), hess_diag.T)
    return pairs.T[None]


def solution(mesh):
    return jax.shard_map(
        on_device,
        mesh=mesh,
        in_specs=(P("aux", "orb", None), P("aux", "orb", None), P()),
        out_specs=P("orb", None, "aux"),
        check_vma=False,
    )
```
